32 devices in a mesh: occ: 4 (over y, x), aux: 8 (over z, core).
Axes of the slice: x: 2, y: 2, z: 4, core: 2. Of those that a mesh axis runs over, the one named last changes fastest.
Arguments:
- integrals: bfloat16 [16384, 16, 256], P(('aux', 'occ')), may hold values from -0.59765625 to 0.59765625
- eps_occ: float32 [1024], replicated, may hold values from -3 to -0.5
- eps_vir: float32 [4096], replicated, may hold values from 0.5 to 4
- src_occ: int32 [4], replicated, may hold values from 0 to 15
- occ_offset: int32 [1], replicated, may hold values from 0 to 1008
- vir_offset: int32 [1], replicated, may hold values from 0 to 3840
Outputs:
- density: bfloat16 [16384, 16, 256], P('aux', 'occ')
The draws below stay inside these ranges and needn't reach their ends.
Inputs may be any that keep to these rules, and one draw needn't show every extreme that they name: `src_occ`: each entry is an occupied index inside the window. `occ_offset`: the window of 16 occupied orbitals lies inside the occupied energies. `vir_offset`: the block of 256 virtual orbitals lies inside the virtual energies.
All inputs are finite; a program needn't handle non-finite values.
Results may differ from the reference program's by a relative error of at most 0.009.
Values may be sent and summed in bfloat16 or wider, within the bound.
No kernel may reach another device: no remote copies, remote signals or barrier semaphores. Data moves between devices by JAX's collectives and lax.ppermute only.
A program may use at most 64 MiB of HBM per device.

```python
import jax
import jax.numpy as jnp
from jax import lax

NAUX = 16384
NOCC = 1024
NVIRT = 4096
NVB = 256
NSRC = 4
NOW = 16
N_AUX = 8


def touch_ends(entries, stream_key, least, largest):
    longest = entries.shape.index(max(entries.shape))
    spots = []
    for shift in (0, 1):
        where = [jax.random.randint(jax.random.fold_in(stream_key, axis), (), 0, length) for axis, length in enumerate(entries.shape)]
        where[longest] = (where[longest] + shift) % entries.shape[longest]
        spots.append(tuple(where))
    return entries.at[spots[0]].set(least).at[spots[1]].set(largest)


def block_scale(rng, dims, shards, least, largest):
    loudness = 1.0
    for dim, parts in shards:
        steps = jax.random.uniform(jax.random.fold_in(jax.random.fold_in(rng, 6), dim), (parts,), jnp.float32, least / len(shards), largest / len(shards))
        loudness = loudness * jnp.repeat(jnp.exp(steps), dims[dim] // parts).reshape((-1,) + (1,) * (len(dims) - 1 - dim))
    return loudness


def centred(rng, dims, width, most, shards=(), dtype=jnp.bfloat16):
    loudness = block_scale(rng, dims, shards, -0.22, 0.18) if shards else 1.0
    values = jax.random.normal(rng, dims, jnp.float32) * width * loudness
    return jnp.minimum(jnp.maximum(values, -most), most).astype(dtype)


def setup_inputs(seed: int = 0) -> dict:
    key_of = jax.random.split(jax.random.key(seed), 7)
    integrals = centred(key_of[0], (NAUX, NOW, NVB), 0.09, 0.59765625, ((0, 32),))
    eps_occ = jnp.clip(jax.random.uniform(key_of[1], (NOCC,), jnp.float32, -3.0, -0.5), -3.0, -0.5)
    eps_vir = jnp.clip(jax.random.uniform(key_of[2], (NVIRT,), jnp.float32, 0.5, 4.0), 0.5, 4.0)
    src_occ = touch_ends(jax.random.randint(key_of[3], (NSRC,), 0, NOW), jax.random.fold_in(key_of[3], 1), 0, NOW - 1).astype(jnp.int32)
    occ_offset = jax.random.randint(key_of[4], (1,), 0, NOCC - NOW + 1).astype(jnp.int32)
    vir_offset = jax.random.randint(key_of[5], (1,), 0, NVIRT - NVB + 1).astype(jnp.int32)
    return {"integrals": integrals, "eps_occ": eps_occ, "eps_vir": eps_vir, "src_occ": src_occ, "occ_offset": occ_offset, "vir_offset": vir_offset}


def reference(integrals, eps_occ, eps_vir, src_occ, occ_offset, vir_offset):
    aux_total, occ_count, virt_count = integrals.shape
    group_rows = aux_total // N_AUX
    grouped = integrals.reshape(N_AUX, group_rows, occ_count * virt_count)
    occ_energy = lax.dynamic_slice_in_dim(eps_occ, occ_offset[0], occ_count)
    vir_energy = lax.dynamic_slice_in_dim(eps_vir, vir_offset[0], virt_count)
    amplitudes = []
    sources = []
    for source_step in range(NSRC):
        src_index = src_occ[source_step]
        source = lax.dynamic_index_in_dim(integrals, src_index, 1, keepdims=False)
        source_groups = source.reshape(N_AUX, group_rows, virt_count)

        def add_group(carry, pair_in):
            block_ints, block_src = pair_in
            term = lax.dot_general(block_ints, block_src, (((0,), (0,)), ((), ())), preferred_element_type=jnp.float32)
            return carry + term, None

        start = jnp.zeros((occ_count * virt_count, virt_count), jnp.float32)
        pair_sum, _ = lax.scan(add_group, start, (grouped, source_groups))
        pair_sum = pair_sum.reshape(occ_count, virt_count, virt_count)
        src_energy = lax.dynamic_index_in_dim(eps_occ, occ_offset[0] + src_index, 0, keepdims=False)
        denom = vir_energy[None, :, None] + vir_energy[None, None, :] - occ_energy[:, None, None] - src_energy
        scaled = (pair_sum / denom).astype(jnp.bfloat16).astype(jnp.float32)
        amplitude = (2.0 * scaled - jnp.transpose(scaled, (0, 2, 1))).astype(jnp.bfloat16)
        amplitudes.append(amplitude.reshape(occ_count * virt_count, virt_count))
        sources.append(source_groups)
    amp_stack = jnp.stack(amplitudes)
    src_stack = jnp.stack(sources, axis=1)

    def density_group(src_group):
        total = jnp.zeros((group_rows, occ_count * virt_count), jnp.float32)
        for source_step in range(NSRC):
            total = total + lax.dot_general(src_group[source_step], amp_stack[source_step], (((1,), (1,)), ((), ())), preferred_element_type=jnp.float32)
        return total.astype(jnp.bfloat16)

    result = lax.map(density_group, src_stack)
    return result.reshape(aux_total, occ_count, virt_count)
```

```python
import functools

import jax
import jax.numpy as jnp
from jax import lax
from jax.experimental import pallas as pl
from jax.experimental.pallas import tpu as pltpu
from jax.sharding import PartitionSpec as P

F32, BF16 = jnp.float32, jnp.bfloat16
VMEM_LIMIT = 48 << 20


def swap(value, axis, size, mask):
    return lax.ppermute(value, axis, [(d, d ^ mask) for d in range(size)])


def whole(shape):
    return pl.BlockSpec(shape, lambda *_: (0,) * len(shape))


def prepare_kernel(counts, src_count, index_ref, src_ref, x_ref, *refs):
    halves, src_t, outs, turned = refs[:2], refs[2], refs[3:-1], refs[-1]
    turned[...] = jnp.swapaxes(x_ref[...], 0, 1)
    width = x_ref.shape[2]
    per_half = src_count // 2
    for s in range(src_count):
        block = turned[src_ref[s]]
        place = pl.ds((s % per_half) * width, width)
        halves[s // per_half][:, place] = block
        src_t[pl.ds(s * width, width), :] = block.T
    spot = 0
    for out, count in zip(outs, counts, strict=True):
        for j in range(count):
            out[j] = turned[index_ref[spot]]
            spot += 1


def prepare(integrals, order, src, counts):
    rows, occ_count, width = integrals.shape
    src_count = src.shape[0]
    step = min(rows, 128)
    half = src_count * width // 2
    shapes = [(rows, half)] * 2 + [(src_count * width, rows)] + [(c, rows, width) for c in counts]
    specs = (
        [pl.BlockSpec((step, half), lambda r, *_: (r, 0))] * 2
        + [pl.BlockSpec((src_count * width, step), lambda r, *_: (0, r))]
        + [pl.BlockSpec((c, step, width), lambda r, *_: (0, r, 0)) for c in counts]
    )
    return pl.pallas_call(
        functools.partial(prepare_kernel, counts, src_count),
        grid_spec=pltpu.PrefetchScalarGridSpec(
            num_scalar_prefetch=2,
            grid=(rows // step,),
            in_specs=[pl.BlockSpec((step, occ_count, width), lambda r, *_: (r, 0, 0))],
            out_specs=specs,
            scratch_shapes=[pltpu.VMEM((occ_count, step, width), BF16)],
        ),
        out_shape=[jax.ShapeDtypeStruct(s, BF16) for s in shapes],
        compiler_params=pltpu.CompilerParams(vmem_limit_bytes=VMEM_LIMIT),
        name="prepare",
    )(order, src, integrals)


def pair_kernel(counts, src_own, src_other, ints_own, ints_other, *outs):
    step = pl.program_id(0)
    total = jnp.dot(src_own[...], ints_own[0], preferred_element_type=F32)
    total += jnp.dot(src_other[...], ints_other[0], preferred_element_type=F32)
    total = total.astype(BF16)
    first = 0
    for out, count in zip(outs, counts, strict=True):

        @pl.when((step >= first) & (step < first + count))
        def _(out=out):
            out[0] = total

        first += count


def pair(src_own, src_other, ints_own, ints_other, counts):
    count, rows, width = ints_own.shape
    tall = src_own.shape[0]
    firsts = [sum(counts[:i]) for i in range(len(counts))]
    ints_spec = pl.BlockSpec((1, rows, width), lambda i: (i, 0, 0))

    def out_spec(first, size):
        return pl.BlockSpec((1, tall, width), lambda i: (jnp.clip(i - first, 0, size - 1), 0, 0))

    return pl.pallas_call(
        functools.partial(pair_kernel, counts),
        grid=(count,),
        in_specs=[whole((tall, rows))] * 2 + [ints_spec] * 2,
        out_specs=[out_spec(f, c) for f, c in zip(firsts, counts, strict=True)],
        out_shape=[jax.ShapeDtypeStruct((c, tall, width), BF16) for c in counts],
        compiler_params=pltpu.CompilerParams(vmem_limit_bytes=VMEM_LIMIT),
        name="pair",
    )(src_own, src_other, ints_own, ints_other)


def amplitude_kernel(denom, *refs):
    parts, out = refs[:-1], refs[-1]
    total = parts[0][...].astype(F32)
    for part in parts[1:]:
        total += part[...].astype(F32)
    scaled = (total / denom[...]).astype(BF16).astype(F32)
    out[...] = (2.0 * scaled - scaled.T).astype(BF16)


def amplitude_of(denom, parts):
    return pl.pallas_call(
        amplitude_kernel,
        out_shape=jax.ShapeDtypeStruct(denom.shape, BF16),
        name="amplitude",
    )(denom, *parts)


def density_kernel(n_occ, chunks, src_count, place, *refs):
    sources, amps = refs[: 2 * n_occ], refs[2 * n_occ : -2]
    out, gathered = refs[-2:]
    step = pl.program_id(0)
    width = out.shape[2]
    depth = sources[0].shape[1]

    @pl.when(step == 0)
    def _():
        spot = 0
        for core in range(2):
            for chunk in range(chunks):
                row = (place[1] if core == 0 else 1 - place[1]) * chunks + chunk
                for s in range(src_count):
                    gathered[row, pl.ds(s * width, width), :] = amps[spot][...]
                    spot += 1

    for k in range(n_occ):

        @pl.when(step == k)
        def _(k=k):
            parts = []
            for i in range(2 * chunks):
                total = jnp.dot(sources[2 * k][...], gathered[i, :depth], preferred_element_type=F32)
                total += jnp.dot(sources[2 * k + 1][...], gathered[i, depth:], preferred_element_type=F32)
                parts.append(total.astype(BF16))
            out[...] = jnp.swapaxes(jnp.stack(parts, axis=0), 0, 1)


def density_of(sources, amps, place, n_occ, chunks):
    rows, depth = sources[0].shape
    width = amps[0].shape[0]
    src_count = 2 * depth // width
    return pl.pallas_call(
        functools.partial(density_kernel, n_occ, chunks, src_count),
        grid_spec=pltpu.PrefetchScalarGridSpec(
            num_scalar_prefetch=1,
            grid=(n_occ,),
            in_specs=[whole((rows, depth))] * len(sources) + [whole((width, width))] * len(amps),
            out_specs=pl.BlockSpec((rows, 2 * chunks, width), lambda k, place: (k ^ place[0], 0, 0)),
            scratch_shapes=[pltpu.VMEM((2 * chunks, 2 * depth, width), BF16)],
        ),
        out_shape=jax.ShapeDtypeStruct((n_occ * rows, 2 * chunks, width), BF16),
        compiler_params=pltpu.CompilerParams(vmem_limit_bytes=VMEM_LIMIT),
        name="density",
    )(place, *sources, *amps)


def halving_groups(n_occ, bits):
    kept, groups = [0], [[0]]
    for bit in reversed(bits):
        sent = [k | bit for k in kept]
        groups.insert(0, sent)
        kept = sent + kept
    return groups


def solution(mesh):
    n_occ, n_aux = mesh.shape["occ"], mesh.shape["aux"]
    occ_bits = [1 << b for b in range(n_occ.bit_length() - 1)]
    n_chip = n_aux // 2

    def local(integrals, eps_occ, eps_vir, src_occ, occ_offset, vir_offset):
        rows, occ_count, width = integrals.shape
        src_count = src_occ.shape[0]
        owned = occ_count // n_occ
        chunks = owned // 2
        my_occ, my_aux = lax.axis_index("occ"), lax.axis_index("aux")
        core, chip = my_aux % 2, my_aux // 2
        src = src_occ[jnp.arange(src_count, dtype=jnp.int32) ^ (chip % src_count)]

        orders = [occ_bits if c % 2 == 0 else occ_bits[::-1] for c in range(chunks)]
        groups = [halving_groups(n_occ, order) for order in orders]
        first = [[(c, k) for k in groups[c][0]] for c in range(chunks)]
        rest = [(c, k) for c in range(chunks) for g in groups[c][1:] for k in g]
        calls = first + [rest]
        blocks = jnp.array([k * owned + c for call in calls for c, k in call], jnp.int32)
        number = (blocks // owned) ^ my_occ
        mine = number * owned + core * chunks + blocks % owned
        theirs = number * owned + (1 - core) * chunks + blocks % owned
        counts = [len(call) for call in calls]
        low, high, src_t, *ints = prepare(integrals, jnp.concatenate([theirs, mine]), src, counts * 2)
        theirs, mine = ints[: len(calls)], ints[len(calls) :]

        src_t_other = swap(src_t, "aux", n_aux, 1)
        other = [swap(v, "aux", n_aux, 1) for v in theirs]

        occ_energy = lax.dynamic_slice_in_dim(
            eps_occ, occ_offset[0] + my_occ * owned + core * chunks, chunks
        )
        vir_energy = lax.dynamic_slice_in_dim(eps_vir, vir_offset[0], width)
        src_energy = lax.dynamic_index_in_dim(eps_occ, occ_offset[0] + src[0], 0, keepdims=False)
        denoms = [
            vir_energy[None, :] + vir_energy[:, None] - occ_energy[c] - src_energy for c in range(chunks)
        ]

        sizes = [[len(g) for g in groups[c]] for c in range(chunks)]
        partial = [[None] * len(groups[c]) for c in range(chunks)]
        for c in range(chunks):
            (partial[c][0],) = pair(src_t, src_t_other, mine[c], other[c], [sizes[c][0]])
        outs = list(pair(src_t, src_t_other, mine[-1], other[-1], sum((sizes[c][1:] for c in range(chunks)), [])))
        for c in range(chunks):
            for g in range(1, len(groups[c])):
                partial[c][g] = outs.pop(0)

        received = [[] for _ in range(chunks)]
        for step in range(len(occ_bits)):
            for c in range(chunks):
                value = partial[c][step]
                if step:
                    value = value.astype(F32)
                    size = sizes[c][step]
                    for past, arrays in enumerate(received[c]):
                        start = sum(sizes[c][past + 1 : step])
                        value += arrays[start : start + size].astype(F32)
                    value = value.astype(BF16)
                received[c].append(swap(value, "occ", n_occ, orders[c][step]))

        halves = {(0, 0): low, (0, 1): high}
        bit_orders = [occ_bits, occ_bits[::-1]]
        held = lax.optimization_barrier((low, high, *[r[-1] for r in received]))
        received = [r[:-1] + [held[2 + c]] for c, r in enumerate(received)]
        for h in range(2):
            have = [0]
            for bit in bit_orders[h]:
                for k in have:
                    halves[k | bit, h] = swap(held[h] if k == 0 else halves[k, h], "occ", n_occ, bit)
                have = have + [k | bit for k in have]

        amps = [[[] for _ in range(chunks)] for _ in range(2)]
        for c in range(chunks):
            total = partial[c][-1][0].astype(F32)
            for arrays in received[c]:
                total += arrays[-1].astype(F32)
            total = total.reshape(src_count, width, width)
            parts = [total[0]]
            for s in range(1, src_count):
                parts.append(swap(total[s].astype(BF16), "aux", n_aux, 2 * s))
            for bit in range(src_count.bit_length() - 1, n_chip.bit_length() - 1):
                value = sum(part.astype(F32) for part in parts)
                parts = [value, swap(value.astype(BF16), "aux", n_aux, 2 << bit)]
            amp = amplitude_of(denoms[c], parts)
            pieces = [amp] + [swap(amp, "aux", n_aux, 2 * s) for s in range(1, src_count)]
            amps[0][c] = pieces
            amps[1][c] = [swap(v, "aux", n_aux, 1) for v in pieces]

        sources = [halves[k, h] for k in range(n_occ) for h in range(2)]
        place = jnp.stack([my_occ, core]).astype(jnp.int32)
        flat = [v for by_core in amps for by_chunk in by_core for v in by_chunk]
        return density_of(sources, flat, place, n_occ, chunks)

    in_specs = (P(("aux", "occ"), None, None), P(), P(), P(), P(), P())
    out_specs = P("aux", "occ", None)
    return jax.shard_map(local, mesh=mesh, in_specs=in_specs, out_specs=out_specs, check_vma=False)
```

```python
import functools

import jax
import jax.numpy as jnp
from jax import lax
from jax.experimental import pallas as pl
from jax.experimental.pallas import tpu as pltpu
from jax.sharding import PartitionSpec as P

F32, BF16 = jnp.float32, jnp.bfloat16
MIB = 1 << 20


def swap(value, axis, size, mask):
    return lax.ppermute(value, axis, [(d, d ^ mask) for d in range(size)])


def whole(shape):
    return pl.BlockSpec(shape, lambda *_: (0,) * len(shape))


def chip_mask(src_count):
    chip = lax.axis_index("aux") // 2
    return (chip % 2) * (src_count // 2) + chip // 2 % 2


def prepare_kernel(n_occ, chunks, src_count, src_ref, x_ref, *refs):
    halves, src_t, theirs, mine, turned = refs[:2], refs[2], refs[3 : 3 + chunks], refs[3 + chunks : -1], refs[-1]
    turned[...] = jnp.swapaxes(x_ref[...], 0, 1)
    width = x_ref.shape[2]
    per_half = src_count // 2
    mask = chip_mask(src_count)
    for s in range(src_count):
        block = turned[src_ref[s ^ mask]]
        place = pl.ds((s % per_half) * width, width)
        halves[s // per_half][:, place] = block
        src_t[pl.ds(s * width, width), :] = block.T
    my_occ, core = lax.axis_index("occ"), lax.axis_index("aux") % 2
    for outs, side in ((theirs, 1 - core), (mine, core)):
        for chunk, out in enumerate(outs):
            for k in range(n_occ):
                out[k] = turned[((k ^ my_occ) * 2 + side) * chunks + chunk]


def prepare(integrals, src, n_occ, chunks):
    rows, occ_count, width = integrals.shape
    src_count = src.shape[0]
    step = min(rows, 128)
    half = src_count * width // 2
    blocks = [(n_occ, rows, width)] * (2 * chunks)
    shapes = [(rows, half)] * 2 + [(src_count * width, rows)] + blocks
    specs = (
        [pl.BlockSpec((step, half), lambda r, *_: (r, 0))] * 2
        + [pl.BlockSpec((src_count * width, step), lambda r, *_: (0, r))]
        + [pl.BlockSpec((n_occ, step, width), lambda r, *_: (0, r, 0)) for _ in blocks]
    )
    return pl.pallas_call(
        functools.partial(prepare_kernel, n_occ, chunks, src_count),
        grid_spec=pltpu.PrefetchScalarGridSpec(
            num_scalar_prefetch=1,
            grid=(rows // step,),
            in_specs=[pl.BlockSpec((step, occ_count, width), lambda r, *_: (r, 0, 0))],
            out_specs=specs,
            scratch_shapes=[pltpu.VMEM((occ_count, step, width), BF16)],
        ),
        out_shape=[jax.ShapeDtypeStruct(s, BF16) for s in shapes],
        compiler_params=pltpu.CompilerParams(vmem_limit_bytes=16 * MIB),
        name="prepare",
    )(src, integrals)


def pair_kernel(src_own, src_other, ints_own, ints_other, *refs):
    out = refs[-1]
    total = jnp.dot(src_own[...], ints_own[0], preferred_element_type=F32)
    total += jnp.dot(src_other[...], ints_other[0], preferred_element_type=F32)
    out[0] = total.astype(BF16)


def pair(src_own, src_other, ints_own, ints_other, pieces, parts, after=()):
    _, rows, width = ints_own.shape
    tall = src_own.shape[0] // parts
    count = len(pieces)
    split = count // 2

    def sequence(column):
        values = [piece[column] for piece in pieces]
        steps = [values[1] - values[0], values[-1] - values[-2]] if split > 1 else [0, 0]
        assert values == [values[i // split * split] + steps[i // split] * (i % split) for i in range(count)]

        def at(i):
            return jnp.where(i < split, values[0] + steps[0] * i, values[split] + steps[1] * (i - split))

        return at

    part, block = sequence(0), sequence(1)
    return pl.pallas_call(
        pair_kernel,
        grid=(count,),
        in_specs=[pl.BlockSpec((tall, rows), lambda i: (part(i), 0))] * 2
        + [pl.BlockSpec((1, rows, width), lambda i: (block(i), 0, 0))] * 2
        + [pl.BlockSpec(memory_space=pl.ANY)] * len(after),
        out_specs=pl.BlockSpec((1, tall, width), lambda i: (i, 0, 0)),
        out_shape=jax.ShapeDtypeStruct((count, tall, width), BF16),
        compiler_params=pltpu.CompilerParams(vmem_limit_bytes=12 * MIB),
        name="pair",
    )(src_own, src_other, ints_own, ints_other, *after)


def add_terms(refs, terms):
    total = None
    for spot, block, first, count in terms:
        value = refs[spot][block, first : first + count, :].astype(F32)
        total = value if total is None else total + value
    return total


def amplitude(total, chunk, chunks, vir, occ, offset, src):
    owner, core = lax.axis_index("occ"), lax.axis_index("aux") % 2
    first = offset[0]
    row = jnp.broadcast_to(vir[...], total.shape)
    denom = row.T + row - occ[first + (owner * 2 + core) * chunks + chunk] - occ[first + src[chip_mask(src.shape[0])]]
    scaled = (total / denom).astype(BF16).astype(F32)
    return 2.0 * scaled - scaled.T


def merge(outputs, energies=None, after=(), through=()):
    arrays, places = [], {}

    def spot(array):
        if id(array) not in places:
            places[id(array)] = len(arrays)
            arrays.append(array)
        return places[id(array)]

    plans = [[[(spot(t[0]), *t[1:]) for t in terms] for terms in blocks] for blocks in outputs]
    shapes = [(len(blocks), blocks[0][0][3], blocks[0][0][0].shape[2]) for blocks in outputs]
    extra = [] if energies is None else list(energies)
    n_in = len(arrays) + len(extra)

    def kernel(*refs):
        outs = refs[n_in + len(after) + len(through) :][: len(outputs)]
        for plan, out in zip(plans, outs, strict=True):
            for j, terms in enumerate(plan):
                total = add_terms(refs, terms)
                if energies is not None:
                    total = amplitude(total, j, len(plan), *refs[len(arrays) : n_in])
                out[j] = total.astype(BF16)

    anywhere = pl.BlockSpec(memory_space=pl.ANY)
    vmem, smem = pl.BlockSpec(memory_space=pltpu.VMEM), pl.BlockSpec(memory_space=pltpu.SMEM)
    results = pl.pallas_call(
        kernel,
        in_specs=[vmem] * len(arrays) + [vmem, smem, smem, smem][: len(extra)] + [anywhere] * (len(after) + len(through)),
        out_specs=[vmem] * len(outputs) + [anywhere] * len(through),
        out_shape=[jax.ShapeDtypeStruct(s, BF16) for s in shapes]
        + [jax.ShapeDtypeStruct(v.shape, v.dtype) for v in through],
        input_output_aliases={n_in + len(after) + i: len(outputs) + i for i in range(len(through))},
        compiler_params=pltpu.CompilerParams(vmem_limit_bytes=12 * MIB),
        name="merge" if energies is None else "amplitude",
    )(*arrays, *extra, *after, *through)
    return results


class Halving:
    def __init__(self, terms, bits, n_occ):
        self.terms, self.bits, self.n_occ = dict(terms), list(bits), n_occ

    def leaving(self):
        return [k for k in sorted(self.terms) if k & self.bits[0]]

    def plan(self):
        return [self.terms[k] for k in self.leaving()]

    def send(self, value):
        leaving, bit = self.leaving(), self.bits.pop(0)
        arrived = swap(value, "occ", self.n_occ, bit)
        for j, k in enumerate(leaving):
            del self.terms[k]
            self.terms[k ^ bit] = self.terms[k ^ bit] + [(arrived, j, 0, value.shape[1])]
        return arrived


def density_kernel(n_occ, chunks, src_count, *refs):
    sources, amps = refs[: 2 * n_occ], refs[2 * n_occ : -2]
    out, gathered = refs[-2:]
    step = pl.program_id(0)
    width = out.shape[2]
    depth = sources[0].shape[1]

    my_core = lax.axis_index("aux") % 2

    @pl.when(step == 0)
    def _():
        spot = 0
        for core in range(2):
            for s in range(src_count):
                for chunk in range(chunks):
                    row = (my_core if core == 0 else 1 - my_core) * chunks + chunk
                    gathered[row, pl.ds(s * width, width), :] = amps[spot][chunk]
                spot += 1

    for k in range(n_occ):

        @pl.when(step == k)
        def _(k=k):
            parts = []
            for i in range(2 * chunks):
                total = jnp.dot(sources[2 * k][...], gathered[i, :depth], preferred_element_type=F32)
                total += jnp.dot(sources[2 * k + 1][...], gathered[i, depth:], preferred_element_type=F32)
                parts.append(total.astype(BF16))
            out[...] = jnp.swapaxes(jnp.stack(parts, axis=0), 0, 1)


def density_of(sources, amps, n_occ, chunks):
    rows, depth = sources[0].shape
    width = amps[0].shape[2]
    src_count = 2 * depth // width
    vmem = pl.BlockSpec(memory_space=pltpu.VMEM)
    return pl.pallas_call(
        functools.partial(density_kernel, n_occ, chunks, src_count),
        grid=(n_occ,),
        in_specs=[vmem] * (len(sources) + len(amps)),
        out_specs=pl.BlockSpec((rows, 2 * chunks, width), lambda k: (k ^ lax.axis_index("occ"), 0, 0)),
        scratch_shapes=[pltpu.VMEM((2 * chunks, 2 * depth, width), BF16)],
        out_shape=jax.ShapeDtypeStruct((n_occ * rows, 2 * chunks, width), BF16),
        compiler_params=pltpu.CompilerParams(vmem_limit_bytes=20 * MIB),
        name="density",
    )(*sources, *amps)


def solution(mesh):
    n_occ, n_aux = mesh.shape["occ"], mesh.shape["aux"]
    occ_bits = [1 << b for b in range(n_occ.bit_length() - 1)]
    n_chip = n_aux // 2

    def local(integrals, eps_occ, eps_vir, src_occ, occ_offset, vir_offset):
        rows, occ_count, width = integrals.shape
        src_count = src_occ.shape[0]
        owned = occ_count // n_occ
        chunks = owned // 2
        near, far = 2, 4
        low, high, src_t, *ints = prepare(integrals, src_occ, n_occ, chunks)
        theirs, mine = ints[:chunks], ints[chunks:]
        low_x = swap(low, "occ", n_occ, occ_bits[0])
        high_y = swap(high, "occ", n_occ, occ_bits[-1])
        src_other = swap(src_t, "aux", n_aux, 1)
        other = [None] * chunks
        for c in reversed(range(chunks)):
            other[c] = swap(theirs[c], "aux", n_aux, 1)

        vir_energy = lax.dynamic_slice_in_dim(eps_vir, vir_offset[0], width).reshape(1, width)

        def product(c, parts, pieces, after=()):
            return pair(src_t, src_other, mine[c], other[c], pieces, parts, after)

        tall = src_count // 2 * width
        small = tall // 2
        half_n = n_occ // 2
        even, odd = list(range(0, n_occ, 2)), list(range(1, n_occ, 2))
        front, back = list(range(half_n)), list(range(half_n, n_occ))
        near_pieces = [
            [(2, k) for k in odd] + [(3, k) for k in back],
            [(2, k) for k in even] + [(3, k) for k in front],
        ]
        near_got = []
        for pieces in near_pieces:
            near_got.append(swap(product(1, 4, pieces), "aux", n_aux, near))
        sent_x = product(0, 2, [(0, k) for k in odd])
        sent_y = product(0, 2, [(1, k) for k in back])
        held = [vir_energy, low_x, high_y]
        kept_x = product(0, 2, [(0, k) for k in even], held)
        kept_y = product(0, 2, [(1, k) for k in front], held)
        first_x = {2 * i: [(kept_x, i, 0, tall)] for i in range(half_n)}
        first_x |= {2 * i + 1: [(sent_x, i, 0, tall)] for i in range(half_n)}
        first_y = {i: [(kept_y, i, 0, tall)] for i in range(half_n)}
        first_y |= {half_n + i: [(sent_y, i, 0, tall)] for i in range(half_n)}
        unit_x, unit_y = Halving(first_x, occ_bits, n_occ), Halving(first_y, occ_bits[::-1], n_occ)
        got_x, got_y = unit_x.send(sent_x), unit_y.send(sent_y)
        while unit_x.bits:
            sent_x, sent_y = merge([unit_x.plan(), unit_y.plan()])
            got_x, got_y = unit_x.send(sent_x), unit_y.send(sent_y)
        near_kept = product(1, 2, [(0, k) for k in range(n_occ)], [sent_x])
        (sent,) = merge([[unit_y.terms[0]]], after=[got_x])
        got = swap(sent, "aux", n_aux, near)
        terms_0 = unit_x.terms[0] + [(got, 0, 0, tall)]

        def rows_of(terms, first, count):
            return [(array, block, start + first, count) for array, block, start, _ in terms]

        both = [{k: [(near_kept, k, small * part, small)] for k in range(n_occ)} for part in range(2)]
        for got, pieces in zip(near_got, near_pieces, strict=True):
            for j, (part, k) in enumerate(pieces):
                both[part - 2][k].append((got, j, 0, small))
        unit_x, unit_y = Halving(both[0], occ_bits, n_occ), Halving(both[1], occ_bits[::-1], n_occ)
        sent_x, sent_y = merge([unit_x.plan(), unit_y.plan()], after=[])
        got_x, got_y = unit_x.send(sent_x), unit_y.send(sent_y)

        (sent_0,) = merge([[rows_of(terms_0, small, small)]])
        got = swap(sent_0, "aux", n_aux, far)
        terms_0 = rows_of(terms_0, 0, small) + [(got, 0, 0, small)]

        while unit_x.bits:
            sent_x, sent_y = merge([unit_x.plan(), unit_y.plan()])
            got_x, got_y = unit_x.send(sent_x), unit_y.send(sent_y)
        sent, low, high, low_x, high_y = merge(
            [[unit_y.terms[0]]], after=[got_x, sent_0], through=[low, high, low_x, high_y]
        )
        low_y = swap(low, "occ", n_occ, occ_bits[-1])
        high_x = swap(high, "occ", n_occ, occ_bits[0])
        got = swap(sent, "aux", n_aux, far)
        terms_1 = unit_x.terms[0] + [(got, 0, 0, small)]

        sums = [terms_0, terms_1]
        for bit in range(2, n_chip.bit_length() - 1):
            (sent,) = merge([sums])
            got = swap(sent, "aux", n_aux, 2 << bit)
            sums = [[(sent, c, 0, small), (got, c, 0, small)] for c in range(chunks)]
        (amp,) = merge([sums], energies=[vir_energy, eps_occ, occ_offset, src_occ])
        halves = {(0, 0): low, (0, 1): high}
        halves[occ_bits[0], 0], halves[occ_bits[-1], 0] = low_x, low_y
        halves[occ_bits[0], 1], halves[occ_bits[-1], 1] = high_x, high_y
        for h, order in enumerate([occ_bits, occ_bits[::-1]]):
            have = [0]
            for bit in order:
                for k in have:
                    if (k | bit, h) not in halves:
                        halves[k | bit, h] = swap(halves[k, h], "occ", n_occ, bit)
                have = have + [k | bit for k in have]

        far_amp = swap(amp, "aux", n_aux, far)
        near_amp = swap(amp, "aux", n_aux, near)
        (far_amp,) = merge([], after=[low_y, high_x], through=[far_amp])
        both_amp = swap(far_amp, "aux", n_aux, near)
        amps = [amp, far_amp, near_amp, both_amp]
        amps += [swap(v, "aux", n_aux, 1) for v in amps]
        sources = [halves[k, h] for k in range(n_occ) for h in range(2)]
        return density_of(sources, amps, n_occ, chunks)

    in_specs = (P(("aux", "occ"), None, None), P(), P(), P(), P(), P())
    out_specs = P("aux", "occ", None)
    return jax.shard_map(local, mesh=mesh, in_specs=in_specs, out_specs=out_specs, check_vma=False)
```

```python
import functools

import jax
import jax.numpy as jnp
from jax import lax
from jax.experimental import pallas as pl
from jax.experimental.pallas import tpu as pltpu
from jax.sharding import PartitionSpec as P

F32, BF16 = jnp.float32, jnp.bfloat16
MIB = 1 << 20


def swap(value, axis, size, mask):
    return lax.ppermute(value, axis, [(d, d ^ mask) for d in range(size)])


def whole(shape):
    return pl.BlockSpec(shape, lambda *_: (0,) * len(shape))


def chip_mask(src_count):
    chip = lax.axis_index("aux") // 2
    return (chip % 2) * (src_count // 2) + chip // 2 % 2


def prepare_kernel(n_occ, chunks, src_count, src_hbm, x_ref, *refs):
    low_a, high_a, src_b, src_t, theirs, mine = *refs[:4], refs[4 : 4 + chunks], refs[4 + chunks : -4]
    arriving, turned, src_ref, arrived = refs[-4:]
    count, step, _, width = arriving.shape
    per_half = src_count // 2
    piece = min(step, src_b.shape[0])
    copies = [
        pltpu.make_async_copy(x_ref.at[pl.ds(r * step, step)], arriving.at[r], arrived.at[r]) for r in range(count)
    ]
    src_copy = pltpu.make_async_copy(src_hbm, src_ref, arrived.at[count])
    src_copy.start()
    for copy in copies:
        copy.start()
    src_copy.wait()
    mask = chip_mask(src_count)
    my_occ, core = lax.axis_index("occ"), lax.axis_index("aux") % 2
    for r, copy in enumerate(copies):
        rows = pl.ds(r * step, step)
        copy.wait()
        turned[...] = jnp.swapaxes(arriving[r], 0, 1)
        for s in range(src_count):
            block = turned[src_ref[s ^ mask]]
            for first in range(0, step, piece):
                second, place = divmod(r * step + first, src_b.shape[0])
                out, column = (src_b, s) if second else (low_a if s < per_half else high_a, s % per_half)
                out[pl.ds(place, piece), pl.ds(column * width, width)] = block[first : first + piece]
            src_t[pl.ds(s * width, width), rows] = block.T
        for outs, side in ((theirs, 1 - core), (mine, core)):
            for chunk, out in enumerate(outs):
                for k in range(n_occ):
                    out[k, rows, :] = turned[((k ^ my_occ) * 2 + side) * chunks + chunk]


def prepare(integrals, src, n_occ, chunks):
    rows, occ_count, width = integrals.shape
    src_count = src.shape[0]
    step = min(rows, 128)
    half = src_count * width // 2
    blocks = [(n_occ, rows, width)] * (2 * chunks)
    shapes = [(rows // 2, half)] * 2 + [(rows // 2, 2 * half)] + [(src_count * width, rows)] + blocks
    vmem = pl.BlockSpec(memory_space=pltpu.VMEM)
    return pl.pallas_call(
        functools.partial(prepare_kernel, n_occ, chunks, src_count),
        in_specs=[pl.BlockSpec(memory_space=pltpu.HBM)] * 2,
        out_specs=[vmem] * len(shapes),
        out_shape=[jax.ShapeDtypeStruct(s, BF16) for s in shapes],
        scratch_shapes=[
            pltpu.VMEM((rows // step, step, occ_count, width), BF16),
            pltpu.VMEM((occ_count, step, width), BF16),
            pltpu.SMEM((src_count,), jnp.int32),
            pltpu.SemaphoreType.DMA((rows // step + 1,)),
        ],
        cost_estimate=pl.CostEstimate(flops=0, bytes_accessed=0, transcendentals=0),
        compiler_params=pltpu.CompilerParams(vmem_limit_bytes=24 * MIB),
        name="prepare",
    )(*(pltpu.with_memory_space_constraint(v, pltpu.HBM) for v in (src, integrals)))


def pair_kernel(pieces, src_own, src_other, ints_own, ints_other, *refs):
    out = refs[-1]
    tall = out.shape[1]
    for j, (part, block) in enumerate(pieces):
        rows = pl.ds(part * tall, tall)
        total = jnp.dot(src_own[rows, :], ints_own[block], preferred_element_type=F32)
        total += jnp.dot(src_other[rows, :], ints_other[block], preferred_element_type=F32)
        out[j] = total.astype(BF16)


def pair(src_own, src_other, ints_own, ints_other, pieces, parts, after=()):
    vmem = pl.BlockSpec(memory_space=pltpu.VMEM)
    tall, width = src_own.shape[0] // parts, ints_own.shape[2]
    return pl.pallas_call(
        functools.partial(pair_kernel, pieces),
        in_specs=[vmem] * 4 + [pl.BlockSpec(memory_space=pl.ANY)] * len(after),
        out_specs=vmem,
        out_shape=jax.ShapeDtypeStruct((len(pieces), tall, width), BF16),
        compiler_params=pltpu.CompilerParams(vmem_limit_bytes=16 * MIB),
        name="pair",
    )(src_own, src_other, ints_own, ints_other, *after)


def add_terms(refs, terms):
    total = None
    for spot, block, first, count in terms:
        value = refs[spot][block, first : first + count, :].astype(F32)
        total = value if total is None else total + value
    return total


def amplitude(total, chunk, chunks, vir, occ, offset, src):
    owner, core = lax.axis_index("occ"), lax.axis_index("aux") % 2
    first = offset[0]
    row = jnp.broadcast_to(vir[...], total.shape)
    denom = row.T + row - occ[first + (owner * 2 + core) * chunks + chunk] - occ[first + src[chip_mask(src.shape[0])]]
    scaled = (total / denom).astype(BF16).astype(F32)
    return 2.0 * scaled - scaled.T


def merge(outputs, energies=None, after=(), through=()):
    arrays, places = [], {}

    def spot(array):
        if id(array) not in places:
            places[id(array)] = len(arrays)
            arrays.append(array)
        return places[id(array)]

    plans = [[[(spot(t[0]), *t[1:]) for t in terms] for terms in blocks] for blocks in outputs]
    shapes = [(len(blocks), blocks[0][0][3], blocks[0][0][0].shape[2]) for blocks in outputs]
    extra = [] if energies is None else list(energies)
    n_in = len(arrays) + len(extra)

    def kernel(*refs):
        outs = refs[n_in + len(after) + len(through) :][: len(outputs)]
        for plan, out in zip(plans, outs, strict=True):
            for j, terms in enumerate(plan):
                total = add_terms(refs, terms)
                if energies is not None:
                    total = amplitude(total, j, len(plan), *refs[len(arrays) : n_in])
                out[j] = total.astype(BF16)

    anywhere = pl.BlockSpec(memory_space=pl.ANY)
    vmem, smem = pl.BlockSpec(memory_space=pltpu.VMEM), pl.BlockSpec(memory_space=pltpu.SMEM)
    results = pl.pallas_call(
        kernel,
        in_specs=[vmem] * len(arrays) + [vmem, smem, smem, smem][: len(extra)] + [anywhere] * (len(after) + len(through)),
        out_specs=[vmem] * len(outputs) + [anywhere] * len(through),
        out_shape=[jax.ShapeDtypeStruct(s, BF16) for s in shapes]
        + [jax.ShapeDtypeStruct(v.shape, v.dtype) for v in through],
        input_output_aliases={n_in + len(after) + i: len(outputs) + i for i in range(len(through))},
        compiler_params=pltpu.CompilerParams(vmem_limit_bytes=12 * MIB),
        name="merge" if energies is None else "amplitude",
    )(*arrays, *extra, *after, *through)
    return results


def spotted(values):
    arrays, spots = [], []
    for array, index in values:
        same = [array is v for v in arrays]
        if not any(same):
            arrays.append(array)
            same.append(True)
        spots.append((same.index(True), index))
    return arrays, spots


def take(refs, spot):
    number, index = spot
    return refs[number][index] if index else refs[number][...]


def cut(array, index):
    return jax.eval_shape(lambda v: v[index], array).shape


def pack_kernel(spots, sizes, *refs):
    outs = refs[-len(sizes) :]
    for out, size in zip(outs, sizes, strict=True):
        for j in range(size):
            out[j] = take(refs, spots[j])
        spots = spots[size:]


def pack(groups, after=()):
    arrays, spots = spotted([v for group in groups for v in group])
    sizes = [len(group) for group in groups]
    shape = cut(*groups[0][0])
    vmem = pl.BlockSpec(memory_space=pltpu.VMEM)
    return pl.pallas_call(
        functools.partial(pack_kernel, spots, sizes),
        in_specs=[vmem] * len(arrays) + [pl.BlockSpec(memory_space=pl.ANY)] * len(after),
        out_specs=[vmem] * len(groups),
        out_shape=[jax.ShapeDtypeStruct((size, *shape), BF16) for size in sizes],
        compiler_params=pltpu.CompilerParams(vmem_limit_bytes=12 * MIB),
        name="pack",
    )(*arrays, *after)


class Halving:
    def __init__(self, terms, bits, n_occ):
        self.terms, self.bits, self.n_occ = dict(terms), list(bits), n_occ

    def leaving(self):
        return [k for k in sorted(self.terms) if k & self.bits[0]]

    def plan(self):
        return [self.terms[k] for k in self.leaving()]

    def send(self, value):
        leaving, bit = self.leaving(), self.bits.pop(0)
        arrived = swap(value, "occ", self.n_occ, bit)
        for j, k in enumerate(leaving):
            del self.terms[k]
            self.terms[k ^ bit] = self.terms[k ^ bit] + [(arrived, j, 0, value.shape[1])]
        return arrived


def source_block(arrays, spots, k):
    low_a, low_b, high_a, high_b = (take(arrays, spot) for spot in spots[4 * k : 4 * k + 4])
    halves = [jnp.concatenate(pair_of, axis=1) for pair_of in ((low_a, high_a), (low_b, high_b))]
    return jnp.concatenate(halves, axis=0)


def gather_amplitudes(amps, chunks, gathered):
    my_core = lax.axis_index("aux") % 2
    steps = len(amps) // 2
    width = gathered.shape[2]
    for spot, amp in enumerate(amps):
        core, s = divmod(spot, steps)
        for chunk in range(chunks):
            row = (my_core if core == 0 else 1 - my_core) * chunks + chunk
            gathered[row, pl.ds(s * width, width), :] = amp[chunk]


def density_first_kernel(n_occ, chunks, spots, count, *refs):
    arrays, amps = refs[:count], refs[count:-2]
    out, gathered = refs[-2:]
    depth, width = gathered.shape[1:]
    gather_amplitudes(amps, chunks, gathered)
    for k in range(n_occ):
        sources = source_block(arrays, spots, k)[:, :depth]
        for i in range(2 * chunks):
            out[k, :, pl.ds(i * width, width)] = jnp.dot(sources, gathered[i], preferred_element_type=F32)


def density_last_kernel(n_occ, chunks, spots, count, *refs):
    arrays, amps, first = refs[:count], refs[count:-3], refs[-3]
    out, gathered = refs[-2:]
    step = pl.program_id(0)
    depth, width = gathered.shape[1:]

    @pl.when(step == 0)
    def _():
        gather_amplitudes(amps, chunks, gathered)

    for k in range(n_occ):

        @pl.when(step == k)
        def _(k=k):
            sources = source_block(arrays, spots, k)[:, -depth:]
            parts = []
            for i in range(2 * chunks):
                total = jnp.dot(sources, gathered[i], preferred_element_type=F32)
                parts.append((total + first[k, :, i * width : (i + 1) * width]).astype(BF16))
            out[...] = jnp.swapaxes(jnp.stack(parts, axis=0), 0, 1)


def density_first(sources, amps, n_occ, chunks):
    arrays, spots = spotted([v for block in sources for v in block])
    rows, width = 2 * cut(*sources[0][0])[0], amps[0][0].shape[2]
    vmem = pl.BlockSpec(memory_space=pltpu.VMEM)
    early = [amp for by_core in amps for amp in by_core]
    return pl.pallas_call(
        functools.partial(density_first_kernel, n_occ, chunks, spots, len(arrays)),
        in_specs=[vmem] * (len(arrays) + len(early)),
        out_specs=vmem,
        scratch_shapes=[pltpu.VMEM((2 * chunks, len(amps[0]) * width, width), BF16)],
        out_shape=jax.ShapeDtypeStruct((n_occ, rows, 2 * chunks * width), F32),
        compiler_params=pltpu.CompilerParams(vmem_limit_bytes=20 * MIB),
        name="density_first",
    )(*arrays, *early)


def density_last(sources, late, first, n_occ, chunks):
    arrays, spots = spotted([v for block in sources for v in block])
    rows, width = 2 * cut(*sources[0][0])[0], late[0].shape[2]
    vmem = pl.BlockSpec(memory_space=pltpu.VMEM)
    return pl.pallas_call(
        functools.partial(density_last_kernel, n_occ, chunks, spots, len(arrays)),
        grid=(n_occ,),
        in_specs=[vmem] * (len(arrays) + len(late) + 1),
        out_specs=pl.BlockSpec((rows, 2 * chunks, width), lambda k: (k ^ lax.axis_index("occ"), 0, 0)),
        scratch_shapes=[pltpu.VMEM((2 * chunks, width, width), BF16)],
        out_shape=jax.ShapeDtypeStruct((n_occ * rows, 2 * chunks, width), BF16),
        compiler_params=pltpu.CompilerParams(vmem_limit_bytes=20 * MIB),
        name="density_last",
    )(*arrays, *late, first)


def solution(mesh):
    n_occ, n_aux = mesh.shape["occ"], mesh.shape["aux"]
    occ_bits = [1 << b for b in range(n_occ.bit_length() - 1)]
    n_chip = n_aux // 2

    def local(integrals, eps_occ, eps_vir, src_occ, occ_offset, vir_offset):
        rows, occ_count, width = integrals.shape
        src_count = src_occ.shape[0]
        owned = occ_count // n_occ
        chunks = owned // 2
        near, far = 2, 4
        low_a, high_a, src_b, src_t, *ints = prepare(integrals, src_occ, n_occ, chunks)
        theirs, mine = ints[:chunks], ints[chunks:]
        columns = low_a.shape[1]
        part_low, part_high = (slice(None), slice(0, columns)), (slice(None), slice(columns, 2 * columns))
        streams = [
            (occ_bits, {0: (low_a, ()), occ_bits[0]: (swap(low_a, "occ", n_occ, occ_bits[0]), ())}),
            (occ_bits[::-1], {0: (high_a, ()), occ_bits[-1]: (swap(high_a, "occ", n_occ, occ_bits[-1]), ())}),
            (occ_bits, {0: (src_b, part_low)}),
            (occ_bits[::-1], {0: (src_b, part_high)}),
        ]
        ahead = [streams[h][1][bit][0] for h, bit in ((0, occ_bits[0]), (1, occ_bits[-1]))]

        def leaving_sources(step):
            groups = {}
            for number, (order, have) in enumerate(streams):
                blocks = [0]
                for bit in order[:step]:
                    blocks = blocks + [k | bit for k in blocks]
                wanted = [(number, k) for k in blocks if k | order[step] not in have]
                groups.setdefault(order[step], []).extend(wanted)
            return groups

        def pack_sources(groups, after=()):
            return pack([[streams[number][1][k] for number, k in group] for group in groups.values()], after)

        def send_sources(groups, packs):
            arrived = [swap(packed, "occ", n_occ, bit) for bit, packed in zip(groups, packs, strict=True)]
            for (bit, group), array in zip(groups.items(), arrived, strict=True):
                for j, (number, k) in enumerate(group):
                    streams[number][1][k | bit] = (array, (j,))
            return arrived

        src_other = swap(src_t, "aux", n_aux, 1)
        other = [None] * chunks
        for c in reversed(range(chunks)):
            other[c] = swap(theirs[c], "aux", n_aux, 1)

        vir_energy = lax.dynamic_slice_in_dim(eps_vir, vir_offset[0], width).reshape(1, width)

        def product(c, parts, pieces, after=()):
            return pair(src_t, src_other, mine[c], other[c], pieces, parts, after)

        tall = src_count // 2 * width
        small = tall // 2
        half_n = n_occ // 2
        even, odd = list(range(0, n_occ, 2)), list(range(1, n_occ, 2))
        front, back = list(range(half_n)), list(range(half_n, n_occ))
        near_pieces = [
            [(2, k) for k in odd] + [(3, k) for k in back],
            [(2, k) for k in even] + [(3, k) for k in front],
        ]
        near_sent = product(1, 4, near_pieces[0])
        near_got = [swap(near_sent, "aux", n_aux, near)]
        sent_x = product(0, 2, [(0, k) for k in odd], [near_sent])
        sent_y = product(0, 2, [(1, k) for k in back], [near_sent, *ahead])
        near_got.append(swap(product(1, 4, near_pieces[1], [sent_x, sent_y]), "aux", n_aux, near))
        held = [vir_energy, near_got[0]]
        kept_x = product(0, 2, [(0, k) for k in even], held)
        kept_y = product(0, 2, [(1, k) for k in front], held)
        first_x = {2 * i: [(kept_x, i, 0, tall)] for i in range(half_n)}
        first_x |= {2 * i + 1: [(sent_x, i, 0, tall)] for i in range(half_n)}
        first_y = {i: [(kept_y, i, 0, tall)] for i in range(half_n)}
        first_y |= {half_n + i: [(sent_y, i, 0, tall)] for i in range(half_n)}
        unit_x, unit_y = Halving(first_x, occ_bits, n_occ), Halving(first_y, occ_bits[::-1], n_occ)
        got_x, got_y = unit_x.send(sent_x), unit_y.send(sent_y)
        while unit_x.bits:
            sent_x, sent_y = merge([unit_x.plan(), unit_y.plan()])
            got_x, got_y = unit_x.send(sent_x), unit_y.send(sent_y)
        near_kept = product(1, 2, [(0, k) for k in range(n_occ)], [sent_x])
        (sent,) = merge([[unit_y.terms[0]]], after=[got_x])
        got = swap(sent, "aux", n_aux, near)
        terms_0 = unit_x.terms[0] + [(got, 0, 0, tall)]

        def rows_of(terms, first, count):
            return [(array, block, start + first, count) for array, block, start, _ in terms]

        both = [{k: [(near_kept, k, small * part, small)] for k in range(n_occ)} for part in range(2)]
        for got, pieces in zip(near_got, near_pieces, strict=True):
            for j, (part, k) in enumerate(pieces):
                both[part - 2][k].append((got, j, 0, small))
        unit_x, unit_y = Halving(both[0], occ_bits, n_occ), Halving(both[1], occ_bits[::-1], n_occ)
        sent_x, sent_y = merge([unit_x.plan(), unit_y.plan()], after=[])
        got_x, got_y = unit_x.send(sent_x), unit_y.send(sent_y)

        while unit_x.bits:
            sent_x, sent_y = merge([unit_x.plan(), unit_y.plan()])
            got_x, got_y = unit_x.send(sent_x), unit_y.send(sent_y)
        sent, src_b = merge(
            [[rows_of(terms_0, small, small), unit_y.terms[0]]],
            after=[got_x],
            through=[src_b],
        )
        got = swap(sent, "aux", n_aux, far)
        terms_0 = rows_of(terms_0, 0, small) + [(got, 0, 0, small)]
        terms_1 = unit_x.terms[0] + [(got, 1, 0, small)]
        for number, part in ((2, part_low), (3, part_high)):
            streams[number][1][0] = (src_b, part)
        for bit in {occ_bits[0], occ_bits[-1]}:
            arrived = swap(src_b, "occ", n_occ, bit)
            streams[2][1][bit], streams[3][1][bit] = (arrived, part_low), (arrived, part_high)
        for step in range(len(occ_bits)):
            groups = leaving_sources(step)
            if any(groups.values()):
                last = send_sources(groups, pack_sources(groups, [got]))

        sums = [terms_0, terms_1]
        for bit in range(2, n_chip.bit_length() - 1):
            (sent,) = merge([sums])
            got = swap(sent, "aux", n_aux, 2 << bit)
            sums = [[(sent, c, 0, small), (got, c, 0, small)] for c in range(chunks)]
        (amp,) = merge([sums], energies=[vir_energy, eps_occ, occ_offset, src_occ])
        far_amp, near_amp = swap(amp, "aux", n_aux, far), swap(amp, "aux", n_aux, near)
        far_amp, near_amp, amp = merge([], through=[far_amp, near_amp, amp])
        both_amp = swap(far_amp, "aux", n_aux, near)
        amps = [amp, far_amp, near_amp]
        other = [swap(v, "aux", n_aux, 1) for v in amps]
        sources = [[streams[number][1][k] for number in (0, 2, 1, 3)] for k in range(n_occ)]
        first = density_first(sources, [amps, other], n_occ, chunks)
        (both_amp,) = merge([], after=[first], through=[both_amp])
        late = [both_amp, swap(both_amp, "aux", n_aux, 1)]
        return density_last(sources, late, first, n_occ, chunks)

    in_specs = (P(("aux", "occ"), None, None), P(), P(), P(), P(), P())
    out_specs = P("aux", "occ", None)
    return jax.shard_map(local, mesh=mesh, in_specs=in_specs, out_specs=out_specs, check_vma=False)
```

```python
import functools

import jax
import jax.numpy as jnp
from jax import lax
from jax.experimental import pallas as pl
from jax.experimental.pallas import tpu as pltpu
from jax.sharding import PartitionSpec as P

F32, BF16 = jnp.float32, jnp.bfloat16
MIB = 1 << 20


def swap(value, axis, size, mask):
    return lax.ppermute(value, axis, [(d, d ^ mask) for d in range(size)])


def whole(shape):
    return pl.BlockSpec(shape, lambda *_: (0,) * len(shape))


def chip_mask(src_count):
    chip = lax.axis_index("aux") // 2
    return (chip % 2) * (src_count // 2) + chip // 2 % 2


def prepare_kernel(n_occ, chunks, src_count, src_hbm, x_ref, *refs):
    quarters, src_t, theirs, mine = refs[:4], refs[4], refs[5 : 5 + chunks], refs[5 + chunks : -4]
    arriving, turned, src_ref, arrived = refs[-4:]
    count, step, _, width = arriving.shape
    per_half = src_count // 2
    piece = min(step, quarters[0].shape[0])
    copies = [
        pltpu.make_async_copy(x_ref.at[pl.ds(r * step, step)], arriving.at[r], arrived.at[r]) for r in range(count)
    ]
    src_copy = pltpu.make_async_copy(src_hbm, src_ref, arrived.at[count])
    src_copy.start()
    for copy in copies:
        copy.start()
    src_copy.wait()
    mask = chip_mask(src_count)
    my_occ, core = lax.axis_index("occ"), lax.axis_index("aux") % 2
    for r, copy in enumerate(copies):
        rows = pl.ds(r * step, step)
        copy.wait()
        turned[...] = jnp.swapaxes(arriving[r], 0, 1)
        for s in range(src_count):
            block = turned[src_ref[s ^ mask]]
            for first in range(0, step, piece):
                number, place = divmod(r * step + first, quarters[0].shape[0])
                out, column = quarters[2 * number + s // per_half], s % per_half
                out[pl.ds(place, piece), pl.ds(column * width, width)] = block[first : first + piece]
            src_t[pl.ds(s * width, width), rows] = block.T
        for outs, side in ((theirs, 1 - core), (mine, core)):
            for chunk, out in enumerate(outs):
                for k in range(n_occ):
                    out[k, rows, :] = turned[((k ^ my_occ) * 2 + side) * chunks + chunk]


def prepare(integrals, src, n_occ, chunks):
    rows, occ_count, width = integrals.shape
    src_count = src.shape[0]
    step = min(rows, 128)
    half = src_count * width // 2
    blocks = [(n_occ, rows, width)] * (2 * chunks)
    shapes = [(rows // 2, half)] * 4 + [(src_count * width, rows)] + blocks
    vmem = pl.BlockSpec(memory_space=pltpu.VMEM)
    return pl.pallas_call(
        functools.partial(prepare_kernel, n_occ, chunks, src_count),
        in_specs=[pl.BlockSpec(memory_space=pltpu.HBM)] * 2,
        out_specs=[vmem] * len(shapes),
        out_shape=[jax.ShapeDtypeStruct(s, BF16) for s in shapes],
        scratch_shapes=[
            pltpu.VMEM((rows // step, step, occ_count, width), BF16),
            pltpu.VMEM((occ_count, step, width), BF16),
            pltpu.SMEM((src_count,), jnp.int32),
            pltpu.SemaphoreType.DMA((rows // step + 1,)),
        ],
        cost_estimate=pl.CostEstimate(flops=0, bytes_accessed=0, transcendentals=0),
        compiler_params=pltpu.CompilerParams(vmem_limit_bytes=24 * MIB),
        name="prepare",
    )(*(pltpu.with_memory_space_constraint(v, pltpu.HBM) for v in (src, integrals)))


def pair_kernel(pieces, src_own, src_other, ints_own, ints_other, *refs):
    out = refs[-1]
    tall = out.shape[1]
    for j, (part, block) in enumerate(pieces):
        rows = pl.ds(part * tall, tall)
        total = jnp.dot(src_own[rows, :], ints_own[block], preferred_element_type=F32)
        total += jnp.dot(src_other[rows, :], ints_other[block], preferred_element_type=F32)
        out[j] = total.astype(BF16)


def pair(src_own, src_other, ints_own, ints_other, pieces, parts, after=()):
    vmem = pl.BlockSpec(memory_space=pltpu.VMEM)
    tall, width = src_own.shape[0] // parts, ints_own.shape[2]
    return pl.pallas_call(
        functools.partial(pair_kernel, pieces),
        in_specs=[vmem] * 4 + [pl.BlockSpec(memory_space=pl.ANY)] * len(after),
        out_specs=vmem,
        out_shape=jax.ShapeDtypeStruct((len(pieces), tall, width), BF16),
        compiler_params=pltpu.CompilerParams(vmem_limit_bytes=16 * MIB),
        name="pair",
    )(src_own, src_other, ints_own, ints_other, *after)


def add_terms(refs, terms):
    total = None
    for spot, block, first, count in terms:
        value = refs[spot][block, first : first + count, :].astype(F32)
        total = value if total is None else total + value
    return total


def occupied(chunk, chunks):
    return (lax.axis_index("occ") * 2 + lax.axis_index("aux") % 2) * chunks + chunk


def amplitude(total, place, vir, occ, offset, src):
    first = offset[0]
    row = jnp.broadcast_to(vir[...], total.shape)
    denom = row.T + row - occ[first + place()] - occ[first + src[chip_mask(src.shape[0])]]
    scaled = (total / denom).astype(BF16).astype(F32)
    return 2.0 * scaled - scaled.T


def merge(outputs, energies=None, chunk=0, chunks=1, after=(), through=()):
    arrays, places = [], {}

    def spot(array):
        if id(array) not in places:
            places[id(array)] = len(arrays)
            arrays.append(array)
        return places[id(array)]

    plans = [[[(spot(t[0]), *t[1:]) for t in terms] for terms in blocks] for blocks in outputs]
    shapes = [(len(blocks), blocks[0][0][3], blocks[0][0][0].shape[2]) for blocks in outputs]
    extra = [] if energies is None else list(energies)
    n_in = len(arrays) + len(extra)

    def kernel(*refs):
        outs = refs[n_in + len(after) + len(through) :][: len(outputs)]
        for plan, out in zip(plans, outs, strict=True):
            for j, terms in enumerate(plan):
                total = add_terms(refs, terms)
                if energies is not None:
                    total = amplitude(total, functools.partial(occupied, chunk + j, chunks), *refs[len(arrays) : n_in])
                out[j] = total.astype(BF16)

    anywhere = pl.BlockSpec(memory_space=pl.ANY)
    vmem, smem = pl.BlockSpec(memory_space=pltpu.VMEM), pl.BlockSpec(memory_space=pltpu.SMEM)
    results = pl.pallas_call(
        kernel,
        in_specs=[vmem] * len(arrays) + [vmem, smem, smem, smem][: len(extra)] + [anywhere] * (len(after) + len(through)),
        out_specs=[vmem] * len(outputs) + [anywhere] * len(through),
        out_shape=[jax.ShapeDtypeStruct(s, BF16) for s in shapes]
        + [jax.ShapeDtypeStruct(v.shape, v.dtype) for v in through],
        input_output_aliases={n_in + len(after) + i: len(outputs) + i for i in range(len(through))},
        compiler_params=pltpu.CompilerParams(vmem_limit_bytes=12 * MIB),
        name="merge" if energies is None else "amplitude",
    )(*arrays, *extra, *after, *through)
    return results


def spotted(values):
    arrays, spots = [], []
    for array, index in values:
        same = [array is v for v in arrays]
        if not any(same):
            arrays.append(array)
            same.append(True)
        spots.append((same.index(True), index))
    return arrays, spots


def take(refs, spot):
    number, index = spot
    return refs[number][index] if index else refs[number][...]


def cut(array, index):
    return jax.eval_shape(lambda v: v[index], array).shape


def pack_kernel(spots, sizes, *refs):
    outs = refs[-len(sizes) :]
    for out, size in zip(outs, sizes, strict=True):
        for j in range(size):
            out[j] = take(refs, spots[j])
        spots = spots[size:]


def pack(groups, after=()):
    arrays, spots = spotted([v for group in groups for v in group])
    sizes = [len(group) for group in groups]
    shape = cut(*groups[0][0])
    vmem = pl.BlockSpec(memory_space=pltpu.VMEM)
    return pl.pallas_call(
        functools.partial(pack_kernel, spots, sizes),
        in_specs=[vmem] * len(arrays) + [pl.BlockSpec(memory_space=pl.ANY)] * len(after),
        out_specs=[vmem] * len(groups),
        out_shape=[jax.ShapeDtypeStruct((size, *shape), BF16) for size in sizes],
        compiler_params=pltpu.CompilerParams(vmem_limit_bytes=12 * MIB),
        name="pack",
    )(*arrays, *after)


class Halving:
    def __init__(self, terms, bits, n_occ):
        self.terms, self.bits, self.n_occ = dict(terms), list(bits), n_occ

    def leaving(self):
        return [k for k in sorted(self.terms) if k & self.bits[0]]

    def plan(self):
        return [self.terms[k] for k in self.leaving()]

    def send(self, value):
        leaving, bit = self.leaving(), self.bits.pop(0)
        arrived = swap(value, "occ", self.n_occ, bit)
        for j, k in enumerate(leaving):
            del self.terms[k]
            self.terms[k ^ bit] = self.terms[k ^ bit] + [(arrived, j, 0, value.shape[1])]
        return arrived


def gather_amplitudes(refs, keys, spots, chunks, gathered):
    width = gathered.shape[2]
    for (core, step, chunk), spot in zip(keys, spots, strict=True):
        gathered[core * chunks + chunk, pl.ds(step * width, width), :] = take(refs, spot)


def density_first_kernel(plan, *refs):
    keys, spots, amp_keys = plan
    arrays, (out, gathered) = refs[:-2], refs[-2:]
    chunks, depth, width = gathered.shape
    gather_amplitudes(arrays, amp_keys, spots[2 * len(keys) :], chunks, gathered)
    rows = out.shape[1] // 2
    for place, (k, part) in enumerate(keys):
        halves = [take(arrays, spot) for spot in spots[2 * place : 2 * place + 2]]
        sources = jnp.concatenate(halves, axis=1)[:, :depth]
        for i in range(chunks):
            total = jnp.dot(sources, gathered[i], preferred_element_type=F32)
            out[k, pl.ds(part * rows, rows), pl.ds(i * width, width)] = total


def density_last_kernel(chunks, plan, early, *refs):
    keys, spots, amp_keys = plan
    arrays, first, (out, gathered, turned) = refs[:-4], refs[-4], refs[-3:]
    step = pl.program_id(0)
    depth, width = gathered.shape[1:]
    rows = out.shape[0] // 2
    my_core = lax.axis_index("aux") % 2

    @pl.when(step == 0)
    def _():
        gather_amplitudes(arrays, amp_keys, spots[2 * len(keys) :], chunks, gathered)

    for place, (k, part) in enumerate(keys):

        @pl.when(step == k)
        def _(place=place, k=k, part=part):
            halves = [take(arrays, spot) for spot in spots[2 * place : 2 * place + 2]]
            sources = jnp.concatenate(halves, axis=1)
            mine = slice(part * rows, (part + 1) * rows)
            for core in range(2):
                for chunk in range(chunks):
                    done = depth - width if core == 0 and (k, part) in early else 0
                    amps = gathered[core * chunks + chunk, done:]
                    total = jnp.dot(sources[:, done:], amps, preferred_element_type=F32)
                    if done:
                        total += first[k, mine, chunk * width : (chunk + 1) * width]
                    turned[(my_core if core == 0 else 1 - my_core) * chunks + chunk] = total.astype(BF16)
            out[mine] = jnp.swapaxes(turned[...], 0, 1)


def density_plan(sources, amps):
    values = [v for halves in sources.values() for v in halves]
    arrays, spots = spotted(values + list(amps.values()))
    rows, columns = cut(*values[0])
    return arrays, (list(sources), spots, list(amps)), 2 * rows, 2 * columns


def density_first(sources, amps, n_occ, chunks):
    arrays, plan, rows, columns = density_plan(sources, amps)
    width = cut(*amps[0, 0, 0])[1]
    vmem = pl.BlockSpec(memory_space=pltpu.VMEM)
    return pl.pallas_call(
        functools.partial(density_first_kernel, plan),
        in_specs=[vmem] * len(arrays),
        out_specs=vmem,
        scratch_shapes=[pltpu.VMEM((chunks, columns - width, width), BF16)],
        out_shape=jax.ShapeDtypeStruct((n_occ, rows, chunks * width), F32),
        compiler_params=pltpu.CompilerParams(vmem_limit_bytes=20 * MIB),
        name="density_first",
    )(*arrays)


def density_last(sources, early, amps, first, n_occ, chunks):
    arrays, plan, rows, columns = density_plan(sources, amps)
    width = cut(*amps[0, 0, 0])[1]
    vmem = pl.BlockSpec(memory_space=pltpu.VMEM)
    return pl.pallas_call(
        functools.partial(density_last_kernel, chunks, plan, early),
        grid=(n_occ,),
        in_specs=[vmem] * (len(arrays) + 1),
        out_specs=pl.BlockSpec((rows, 2 * chunks, width), lambda k: (k ^ lax.axis_index("occ"), 0, 0)),
        scratch_shapes=[
            pltpu.VMEM((2 * chunks, columns, width), BF16),
            pltpu.VMEM((2 * chunks, rows // 2, width), BF16),
        ],
        out_shape=jax.ShapeDtypeStruct((n_occ * rows, 2 * chunks, width), BF16),
        compiler_params=pltpu.CompilerParams(vmem_limit_bytes=20 * MIB),
        name="density_last",
    )(*arrays, first)


def solution(mesh):
    n_occ, n_aux = mesh.shape["occ"], mesh.shape["aux"]
    occ_bits = [1 << b for b in range(n_occ.bit_length() - 1)]
    n_chip = n_aux // 2

    def local(integrals, eps_occ, eps_vir, src_occ, occ_offset, vir_offset):
        rows, occ_count, width = integrals.shape
        src_count = src_occ.shape[0]
        owned = occ_count // n_occ
        chunks = owned // 2
        near, far = 2, 4
        low_a, high_a, low_b, high_b, src_t, *ints = prepare(integrals, src_occ, n_occ, chunks)
        theirs, mine = ints[:chunks], ints[chunks:]
        orders = [occ_bits, occ_bits[::-1]] * 2
        streams = [{0: (value, ())} for value in (low_a, high_a, low_b, high_b)]
        for order, have in zip(orders[:2], streams[:2], strict=True):
            have[order[0]] = (swap(have[0][0], "occ", n_occ, order[0]), ())
        ahead = [have[order[0]][0] for order, have in zip(orders[:2], streams[:2], strict=True)]

        def leaving_sources():
            groups = {}
            for number, (order, have) in enumerate(zip(orders, streams, strict=True)):
                blocks = [0]
                for bit in order:
                    wanted = [(number, k) for k in blocks if k in have and k | bit not in have]
                    if wanted:
                        groups.setdefault(bit, []).extend(wanted)
                    blocks = blocks + [k | bit for k in blocks]
            return groups

        def pack_sources(groups, after=()):
            return pack([[streams[number][k] for number, k in group] for group in groups.values()], after)

        def send_sources(groups, packs):
            arrived = [swap(packed, "occ", n_occ, bit) for bit, packed in zip(groups, packs, strict=True)]
            for (bit, group), array in zip(groups.items(), arrived, strict=True):
                for j, (number, k) in enumerate(group):
                    streams[number][k | bit] = (array, (j,))

        src_other = swap(src_t, "aux", n_aux, 1)
        other = [None] * chunks
        for c in reversed(range(chunks)):
            other[c] = swap(theirs[c], "aux", n_aux, 1)

        vir_energy = lax.dynamic_slice_in_dim(eps_vir, vir_offset[0], width).reshape(1, width)

        def product(c, parts, pieces, after=()):
            return pair(src_t, src_other, mine[c], other[c], pieces, parts, after)

        tall = src_count // 2 * width
        small = tall // 2
        half_n = n_occ // 2
        even, odd = list(range(0, n_occ, 2)), list(range(1, n_occ, 2))
        front, back = list(range(half_n)), list(range(half_n, n_occ))
        near_pieces = [
            [(2, k) for k in odd] + [(3, k) for k in back],
            [(2, k) for k in even] + [(3, k) for k in front],
        ]
        near_sent = product(1, 4, near_pieces[0])
        near_got = [swap(near_sent, "aux", n_aux, near)]
        sent_x = product(0, 2, [(0, k) for k in odd], [near_sent])
        sent_y = product(0, 2, [(1, k) for k in back], [near_sent, *ahead])
        near_got.append(swap(product(1, 4, near_pieces[1], [sent_x, sent_y]), "aux", n_aux, near))
        groups = leaving_sources()
        packs = pack_sources(groups)
        held = [vir_energy, near_got[0]]
        kept_x = product(0, 2, [(0, k) for k in even], held)
        kept_y = product(0, 2, [(1, k) for k in front], held)
        first_x = {2 * i: [(kept_x, i, 0, tall)] for i in range(half_n)}
        first_x |= {2 * i + 1: [(sent_x, i, 0, tall)] for i in range(half_n)}
        first_y = {i: [(kept_y, i, 0, tall)] for i in range(half_n)}
        first_y |= {half_n + i: [(sent_y, i, 0, tall)] for i in range(half_n)}
        unit_x, unit_y = Halving(first_x, occ_bits, n_occ), Halving(first_y, occ_bits[::-1], n_occ)
        got_x, got_y = unit_x.send(sent_x), unit_y.send(sent_y)
        while unit_x.bits:
            sent_x, sent_y = merge([unit_x.plan(), unit_y.plan()])
            got_x, got_y = unit_x.send(sent_x), unit_y.send(sent_y)
        near_kept = product(1, 2, [(0, k) for k in range(n_occ)], [sent_x])
        (sent,) = merge([[unit_y.terms[0]]], after=[got_x])
        got = swap(sent, "aux", n_aux, near)
        terms_0 = unit_x.terms[0] + [(got, 0, 0, tall)]

        def rows_of(terms, first, count):
            return [(array, block, start + first, count) for array, block, start, _ in terms]

        both = [{k: [(near_kept, k, small * part, small)] for k in range(n_occ)} for part in range(2)]
        for got, pieces in zip(near_got, near_pieces, strict=True):
            for j, (part, k) in enumerate(pieces):
                both[part - 2][k].append((got, j, 0, small))
        unit_x, unit_y = Halving(both[0], occ_bits, n_occ), Halving(both[1], occ_bits[::-1], n_occ)
        sent_x, sent_y = merge([unit_x.plan(), unit_y.plan()], after=[])
        got_x, got_y = unit_x.send(sent_x), unit_y.send(sent_y)

        (sent_0,) = merge([[rows_of(terms_0, small, small)]])
        got_0 = swap(sent_0, "aux", n_aux, far)
        terms_0 = rows_of(terms_0, 0, small) + [(got_0, 0, 0, small)]

        while unit_x.bits:
            sent_x, sent_y = merge([unit_x.plan(), unit_y.plan()])
            got_x, got_y = unit_x.send(sent_x), unit_y.send(sent_y)
        sent_1, *packs = merge([[unit_y.terms[0]]], after=[got_x, sent_0], through=packs)
        got_1 = swap(sent_1, "aux", n_aux, far)
        terms_1 = unit_x.terms[0] + [(got_1, 0, 0, small)]

        send_sources(groups, packs)
        while groups := leaving_sources():
            soon = [dict(have) for have in streams]
            send_sources(groups, pack_sources(groups))
        early, late_rows = [], []
        for k in range(n_occ):
            for part in range(2):
                (early if all(k in soon[2 * part + h] for h in range(2)) else late_rows).append((k, part))

        energies = [vir_energy, eps_occ, occ_offset, src_occ]
        sums = [terms_0, terms_1]
        for bit in range(2, n_chip.bit_length() - 1):
            (sent,) = merge([sums])
            got = swap(sent, "aux", n_aux, 2 << bit)
            sums = [[(sent, c, 0, small), (got, c, 0, small)] for c in range(chunks)]
        (amp,) = merge([sums], energies=energies, chunks=chunks)
        far_amp, near_amp = swap(amp, "aux", n_aux, far), swap(amp, "aux", n_aux, near)
        both_amp = swap(far_amp, "aux", n_aux, near)
        amps = {
            (0, step, c): (value, (c,))
            for step, value in enumerate([amp, far_amp, near_amp, both_amp])
            for c in range(chunks)
        }
        sources = {(k, part): [streams[2 * part + h][k] for h in range(2)] for k in range(n_occ) for part in range(2)}
        known = {key: value for key, value in amps.items() if key[1] < src_count - 1}
        first = density_first({key: sources[key] for key in early}, known, n_occ, chunks)
        last_sources = [streams[2 * part + h][k] for k, part in late_rows for h in range(2)]
        own = list(amps)
        (packed,) = pack([[amps[key] for key in own]], [first, *spotted(last_sources)[0]])
        arrived = swap(packed, "aux", n_aux, 1)
        for j, (_, step, c) in enumerate(own):
            amps[1, step, c] = (arrived, (j,))
        return density_last(sources, set(early), amps, first, n_occ, chunks)

    in_specs = (P(("aux", "occ"), None, None), P(), P(), P(), P(), P())
    out_specs = P("aux", "occ", None)
    return jax.shard_map(local, mesh=mesh, in_specs=in_specs, out_specs=out_specs, check_vma=False)
```

```python
import functools

import jax
import jax.numpy as jnp
from jax import lax
from jax.experimental import pallas as pl
from jax.experimental.pallas import tpu as pltpu
from jax.sharding import PartitionSpec as P

F32, BF16 = jnp.float32, jnp.bfloat16
MIB = 1 << 20


def swap(value, axis, size, mask):
    return lax.ppermute(value, axis, [(d, d ^ mask) for d in range(size)])


def whole(shape):
    return pl.BlockSpec(shape, lambda *_: (0,) * len(shape))


def chip_mask(src_count):
    chip = lax.axis_index("aux") // 2
    return (chip % 2) * (src_count // 2) + chip // 2 % 2


def prepare_kernel(n_occ, chunks, src_count, src_hbm, x_ref, *refs):
    quarters, src_t, theirs, mine = refs[:4], refs[4], refs[5 : 5 + chunks], refs[5 + chunks : -4]
    arriving, turned, src_ref, arrived = refs[-4:]
    count, step, _, width = arriving.shape
    per_half = src_count // 2
    piece = min(step, quarters[0].shape[0])
    copies = [
        pltpu.make_async_copy(x_ref.at[pl.ds(r * step, step)], arriving.at[r], arrived.at[r]) for r in range(count)
    ]
    src_copy = pltpu.make_async_copy(src_hbm, src_ref, arrived.at[count])
    src_copy.start()
    for copy in copies:
        copy.start()
    src_copy.wait()
    mask = chip_mask(src_count)
    my_occ, core = lax.axis_index("occ"), lax.axis_index("aux") % 2
    for r, copy in enumerate(copies):
        rows = pl.ds(r * step, step)
        copy.wait()
        turned[...] = jnp.swapaxes(arriving[r], 0, 1)
        for s in range(src_count):
            block = turned[src_ref[s ^ mask]]
            for first in range(0, step, piece):
                number, place = divmod(r * step + first, quarters[0].shape[0])
                out, column = quarters[2 * number + s // per_half], s % per_half
                out[pl.ds(place, piece), pl.ds(column * width, width)] = block[first : first + piece]
            src_t[pl.ds(s * width, width), rows] = block.T
        for outs, side in ((theirs, 1 - core), (mine, core)):
            for chunk, out in enumerate(outs):
                for k in range(n_occ):
                    out[k, rows, :] = turned[((k ^ my_occ) * 2 + side) * chunks + chunk]


def prepare(integrals, src, n_occ, chunks):
    rows, occ_count, width = integrals.shape
    src_count = src.shape[0]
    step = min(rows, 128)
    half = src_count * width // 2
    blocks = [(n_occ, rows, width)] * (2 * chunks)
    shapes = [(rows // 2, half)] * 4 + [(src_count * width, rows)] + blocks
    vmem = pl.BlockSpec(memory_space=pltpu.VMEM)
    return pl.pallas_call(
        functools.partial(prepare_kernel, n_occ, chunks, src_count),
        in_specs=[pl.BlockSpec(memory_space=pltpu.HBM)] * 2,
        out_specs=[vmem] * len(shapes),
        out_shape=[jax.ShapeDtypeStruct(s, BF16) for s in shapes],
        scratch_shapes=[
            pltpu.VMEM((rows // step, step, occ_count, width), BF16),
            pltpu.VMEM((occ_count, step, width), BF16),
            pltpu.SMEM((src_count,), jnp.int32),
            pltpu.SemaphoreType.DMA((rows // step + 1,)),
        ],
        cost_estimate=pl.CostEstimate(flops=0, bytes_accessed=0, transcendentals=0),
        compiler_params=pltpu.CompilerParams(vmem_limit_bytes=24 * MIB),
        name="prepare",
    )(*(pltpu.with_memory_space_constraint(v, pltpu.HBM) for v in (src, integrals)))


def pair_kernel(pieces, src_own, src_other, ints_own, ints_other, *refs):
    out = refs[-1]
    tall = out.shape[1]
    for j, (part, block) in enumerate(pieces):
        rows = pl.ds(part * tall, tall)
        total = jnp.dot(src_own[rows, :], ints_own[block], preferred_element_type=F32)
        total += jnp.dot(src_other[rows, :], ints_other[block], preferred_element_type=F32)
        out[j] = total.astype(BF16)


def pair(src_own, src_other, ints_own, ints_other, pieces, parts, after=()):
    vmem = pl.BlockSpec(memory_space=pltpu.VMEM)
    tall, width = src_own.shape[0] // parts, ints_own.shape[2]
    return pl.pallas_call(
        functools.partial(pair_kernel, pieces),
        in_specs=[vmem] * 4 + [pl.BlockSpec(memory_space=pl.ANY)] * len(after),
        out_specs=vmem,
        out_shape=jax.ShapeDtypeStruct((len(pieces), tall, width), BF16),
        compiler_params=pltpu.CompilerParams(vmem_limit_bytes=16 * MIB),
        name="pair",
    )(src_own, src_other, ints_own, ints_other, *after)


def add_terms(refs, terms):
    total = None
    for spot, block, first, count in terms:
        value = refs[spot][block, first : first + count, :].astype(F32)
        total = value if total is None else total + value
    return total


def occupied(chunk, chunks):
    return (lax.axis_index("occ") * 2 + lax.axis_index("aux") % 2) * chunks + chunk


def amplitude(total, place, vir, occ, offset, src):
    first = offset[0]
    row = jnp.broadcast_to(vir[...], total.shape)
    denom = row.T + row - occ[first + place()] - occ[first + src[chip_mask(src.shape[0])]]
    scaled = (total / denom).astype(BF16).astype(F32)
    return 2.0 * scaled - scaled.T


def merge(outputs, energies=None, chunk=0, chunks=1, after=(), through=()):
    arrays, places = [], {}

    def spot(array):
        if id(array) not in places:
            places[id(array)] = len(arrays)
            arrays.append(array)
        return places[id(array)]

    plans = [[[(spot(t[0]), *t[1:]) for t in terms] for terms in blocks] for blocks in outputs]
    shapes = [(len(blocks), blocks[0][0][3], blocks[0][0][0].shape[2]) for blocks in outputs]
    extra = [] if energies is None else list(energies)
    n_in = len(arrays) + len(extra)

    def kernel(*refs):
        outs = refs[n_in + len(after) + len(through) :][: len(outputs)]
        for plan, out in zip(plans, outs, strict=True):
            for j, terms in enumerate(plan):
                total = add_terms(refs, terms)
                if energies is not None:
                    total = amplitude(total, functools.partial(occupied, chunk + j, chunks), *refs[len(arrays) : n_in])
                out[j] = total.astype(BF16)

    anywhere = pl.BlockSpec(memory_space=pl.ANY)
    vmem, smem = pl.BlockSpec(memory_space=pltpu.VMEM), pl.BlockSpec(memory_space=pltpu.SMEM)
    results = pl.pallas_call(
        kernel,
        in_specs=[vmem] * len(arrays) + [vmem, smem, smem, smem][: len(extra)] + [anywhere] * (len(after) + len(through)),
        out_specs=[vmem] * len(outputs) + [anywhere] * len(through),
        out_shape=[jax.ShapeDtypeStruct(s, BF16) for s in shapes]
        + [jax.ShapeDtypeStruct(v.shape, v.dtype) for v in through],
        input_output_aliases={n_in + len(after) + i: len(outputs) + i for i in range(len(through))},
        compiler_params=pltpu.CompilerParams(vmem_limit_bytes=12 * MIB),
        name="merge" if energies is None else "amplitude",
    )(*arrays, *extra, *after, *through)
    return results


def spotted(values):
    arrays, spots = [], []
    for array, index in values:
        same = [array is v for v in arrays]
        if not any(same):
            arrays.append(array)
            same.append(True)
        spots.append((same.index(True), index))
    return arrays, spots


def take(refs, spot):
    number, index = spot
    return refs[number][index] if index else refs[number][...]


def cut(array, index):
    return jax.eval_shape(lambda v: v[index], array).shape


def pack_kernel(spots, sizes, *refs):
    outs = refs[-len(sizes) :]
    for out, size in zip(outs, sizes, strict=True):
        for j in range(size):
            out[j] = take(refs, spots[j])
        spots = spots[size:]


def pack(groups, after=()):
    arrays, spots = spotted([v for group in groups for v in group])
    sizes = [len(group) for group in groups]
    shape = cut(*groups[0][0])
    vmem = pl.BlockSpec(memory_space=pltpu.VMEM)
    return pl.pallas_call(
        functools.partial(pack_kernel, spots, sizes),
        in_specs=[vmem] * len(arrays) + [pl.BlockSpec(memory_space=pl.ANY)] * len(after),
        out_specs=[vmem] * len(groups),
        out_shape=[jax.ShapeDtypeStruct((size, *shape), BF16) for size in sizes],
        compiler_params=pltpu.CompilerParams(vmem_limit_bytes=12 * MIB),
        name="pack",
    )(*arrays, *after)


class Halving:
    def __init__(self, terms, bits, n_occ):
        self.terms, self.bits, self.n_occ = dict(terms), list(bits), n_occ

    def leaving(self):
        return [k for k in sorted(self.terms) if k & self.bits[0]]

    def plan(self):
        return [self.terms[k] for k in self.leaving()]

    def send(self, value):
        leaving, bit = self.leaving(), self.bits.pop(0)
        arrived = swap(value, "occ", self.n_occ, bit)
        for j, k in enumerate(leaving):
            del self.terms[k]
            self.terms[k ^ bit] = self.terms[k ^ bit] + [(arrived, j, 0, value.shape[1])]
        return arrived


def gather_amplitudes(refs, keys, spots, chunks, gathered):
    width = gathered.shape[2]
    for (core, step, chunk), spot in zip(keys, spots, strict=True):
        gathered[core * chunks + chunk, pl.ds(step * width, width), :] = take(refs, spot)


def density_first_kernel(plan, *refs):
    keys, spots, amp_keys = plan
    arrays, (out, gathered) = refs[:-2], refs[-2:]
    chunks, depth, width = gathered.shape
    gather_amplitudes(arrays, amp_keys, spots[2 * len(keys) :], chunks, gathered)
    rows = out.shape[1] // 2
    for place, (k, part) in enumerate(keys):
        halves = [take(arrays, spot) for spot in spots[2 * place : 2 * place + 2]]
        sources = jnp.concatenate(halves, axis=1)[:, :depth]
        for i in range(chunks):
            total = jnp.dot(sources, gathered[i], preferred_element_type=F32)
            out[k, pl.ds(part * rows, rows), pl.ds(i * width, width)] = total


def density_last_kernel(chunks, plan, early, *refs):
    keys, spots, amp_keys = plan
    arrays, first, (out, gathered, turned) = refs[:-4], refs[-4], refs[-3:]
    step = pl.program_id(0)
    depth, width = gathered.shape[1:]
    rows = out.shape[0] // 2
    my_core = lax.axis_index("aux") % 2

    @pl.when(step == 0)
    def _():
        gather_amplitudes(arrays, amp_keys, spots[2 * len(keys) :], chunks, gathered)

    for place, (k, part) in enumerate(keys):

        @pl.when(step == k)
        def _(place=place, k=k, part=part):
            halves = [take(arrays, spot) for spot in spots[2 * place : 2 * place + 2]]
            sources = jnp.concatenate(halves, axis=1)
            mine = slice(part * rows, (part + 1) * rows)
            for core in range(2):
                for chunk in range(chunks):
                    done = depth - width if core == 0 and (k, part) in early else 0
                    amps = gathered[core * chunks + chunk, done:]
                    total = jnp.dot(sources[:, done:], amps, preferred_element_type=F32)
                    if done:
                        total += first[k, mine, chunk * width : (chunk + 1) * width]
                    turned[(my_core if core == 0 else 1 - my_core) * chunks + chunk] = total.astype(BF16)
            out[mine] = jnp.swapaxes(turned[...], 0, 1)


def density_plan(sources, amps):
    values = [v for halves in sources.values() for v in halves]
    arrays, spots = spotted(values + list(amps.values()))
    rows, columns = cut(*values[0])
    return arrays, (list(sources), spots, list(amps)), 2 * rows, 2 * columns


def density_first(sources, amps, n_occ, chunks):
    arrays, plan, rows, columns = density_plan(sources, amps)
    width = cut(*amps[0, 0, 0])[1]
    vmem = pl.BlockSpec(memory_space=pltpu.VMEM)
    return pl.pallas_call(
        functools.partial(density_first_kernel, plan),
        in_specs=[vmem] * len(arrays),
        out_specs=vmem,
        scratch_shapes=[pltpu.VMEM((chunks, columns - width, width), BF16)],
        out_shape=jax.ShapeDtypeStruct((n_occ, rows, chunks * width), F32),
        compiler_params=pltpu.CompilerParams(vmem_limit_bytes=20 * MIB),
        name="density_first",
    )(*arrays)


def density_last(sources, early, amps, first, n_occ, chunks):
    arrays, plan, rows, columns = density_plan(sources, amps)
    width = cut(*amps[0, 0, 0])[1]
    vmem = pl.BlockSpec(memory_space=pltpu.VMEM)
    return pl.pallas_call(
        functools.partial(density_last_kernel, chunks, plan, early),
        grid=(n_occ,),
        in_specs=[vmem] * (len(arrays) + 1),
        out_specs=pl.BlockSpec((rows, 2 * chunks, width), lambda k: (k ^ lax.axis_index("occ"), 0, 0)),
        scratch_shapes=[
            pltpu.VMEM((2 * chunks, columns, width), BF16),
            pltpu.VMEM((2 * chunks, rows // 2, width), BF16),
        ],
        out_shape=jax.ShapeDtypeStruct((n_occ * rows, 2 * chunks, width), BF16),
        compiler_params=pltpu.CompilerParams(vmem_limit_bytes=20 * MIB),
        name="density_last",
    )(*arrays, first)


def solution(mesh):
    n_occ, n_aux = mesh.shape["occ"], mesh.shape["aux"]
    occ_bits = [1 << b for b in range(n_occ.bit_length() - 1)]
    n_chip = n_aux // 2

    def local(integrals, eps_occ, eps_vir, src_occ, occ_offset, vir_offset):
        rows, occ_count, width = integrals.shape
        src_count = src_occ.shape[0]
        owned = occ_count // n_occ
        chunks = owned // 2
        near, far = 2, 4
        low_a, high_a, low_b, high_b, src_t, *ints = prepare(integrals, src_occ, n_occ, chunks)
        theirs, mine = ints[:chunks], ints[chunks:]
        orders = [occ_bits, occ_bits[::-1]] * 2
        streams = [{0: (value, ())} for value in (low_a, high_a, low_b, high_b)]
        for order, have in zip(orders[:2], streams[:2], strict=True):
            have[order[0]] = (swap(have[0][0], "occ", n_occ, order[0]), ())
        ahead = [have[order[0]][0] for order, have in zip(orders[:2], streams[:2], strict=True)]

        def leaving_sources():
            groups = {}
            for number, (order, have) in enumerate(zip(orders, streams, strict=True)):
                blocks = [0]
                for bit in order:
                    wanted = [(number, k) for k in blocks if k in have and k | bit not in have]
                    if wanted:
                        groups.setdefault(bit, []).extend(wanted)
                    blocks = blocks + [k | bit for k in blocks]
            return groups

        def pack_sources(groups, after=()):
            return pack([[streams[number][k] for number, k in group] for group in groups.values()], after)

        def send_sources(groups, packs):
            arrived = [swap(packed, "occ", n_occ, bit) for bit, packed in zip(groups, packs, strict=True)]
            for (bit, group), array in zip(groups.items(), arrived, strict=True):
                for j, (number, k) in enumerate(group):
                    streams[number][k | bit] = (array, (j,))

        src_other = swap(src_t, "aux", n_aux, 1)
        other = [None] * chunks
        for c in reversed(range(chunks)):
            other[c] = swap(theirs[c], "aux", n_aux, 1)

        vir_energy = lax.dynamic_slice_in_dim(eps_vir, vir_offset[0], width).reshape(1, width)

        def product(c, parts, pieces, after=()):
            return pair(src_t, src_other, mine[c], other[c], pieces, parts, after)

        tall = src_count // 2 * width
        small = tall // 2
        half_n = n_occ // 2
        even, odd = list(range(0, n_occ, 2)), list(range(1, n_occ, 2))
        front, back = list(range(half_n)), list(range(half_n, n_occ))
        near_pieces = [
            [(2, k) for k in odd] + [(3, k) for k in back],
            [(2, k) for k in even] + [(3, k) for k in front],
        ]
        near_sent = product(1, 4, near_pieces[0])
        near_got = [swap(near_sent, "aux", n_aux, near)]
        sent_x = product(0, 2, [(0, k) for k in odd], [near_sent])
        sent_y = product(0, 2, [(1, k) for k in back], [near_sent, *ahead])
        near_got.append(swap(product(1, 4, near_pieces[1], [sent_x, sent_y]), "aux", n_aux, near))
        groups = leaving_sources()
        packs = pack_sources(groups)
        held = [near_got[0]]
        kept_x = product(0, 2, [(0, k) for k in even], held)
        kept_y = product(0, 2, [(1, k) for k in front], held)
        first_x = {2 * i: [(kept_x, i, 0, tall)] for i in range(half_n)}
        first_x |= {2 * i + 1: [(sent_x, i, 0, tall)] for i in range(half_n)}
        first_y = {i: [(kept_y, i, 0, tall)] for i in range(half_n)}
        first_y |= {half_n + i: [(sent_y, i, 0, tall)] for i in range(half_n)}
        unit_x, unit_y = Halving(first_x, occ_bits, n_occ), Halving(first_y, occ_bits[::-1], n_occ)
        got_x, got_y = unit_x.send(sent_x), unit_y.send(sent_y)
        while unit_x.bits:
            sent_x, sent_y = merge([unit_x.plan(), unit_y.plan()])
            got_x, got_y = unit_x.send(sent_x), unit_y.send(sent_y)
        near_kept = product(1, 2, [(0, k) for k in range(n_occ)], [sent_x])
        (sent,) = merge([[unit_y.terms[0]]], after=[got_x])
        got = swap(sent, "aux", n_aux, near)
        terms_0 = unit_x.terms[0] + [(got, 0, 0, tall)]

        def rows_of(terms, first, count):
            return [(array, block, start + first, count) for array, block, start, _ in terms]

        both = [{k: [(near_kept, k, small * part, small)] for k in range(n_occ)} for part in range(2)]
        for got, pieces in zip(near_got, near_pieces, strict=True):
            for j, (part, k) in enumerate(pieces):
                both[part - 2][k].append((got, j, 0, small))
        unit_x, unit_y = Halving(both[0], occ_bits, n_occ), Halving(both[1], occ_bits[::-1], n_occ)
        sent_x, sent_y = merge([unit_x.plan(), unit_y.plan()], after=[])
        got_x, got_y = unit_x.send(sent_x), unit_y.send(sent_y)

        (sent_0,) = merge([[rows_of(terms_0, small, small)]])
        got_0 = swap(sent_0, "aux", n_aux, far)
        terms_0 = rows_of(terms_0, 0, small) + [(got_0, 0, 0, small)]

        while unit_x.bits:
            sent_x, sent_y = merge([unit_x.plan(), unit_y.plan()])
            got_x, got_y = unit_x.send(sent_x), unit_y.send(sent_y)
        sent_1, *packs = merge([[unit_y.terms[0]]], after=[got_x, sent_0], through=packs)
        got_1 = swap(sent_1, "aux", n_aux, far)
        terms_1 = unit_x.terms[0] + [(got_1, 0, 0, small)]

        send_sources(groups, packs)
        while groups := leaving_sources():
            soon = [dict(have) for have in streams]
            send_sources(groups, pack_sources(groups))
        early = [(k, part) for k in range(n_occ) for part in range(2)]
        late_rows = []

        energies = [vir_energy, eps_occ, occ_offset, src_occ]
        sums = [terms_0, terms_1]
        for bit in range(2, n_chip.bit_length() - 1):
            (sent,) = merge([sums])
            got = swap(sent, "aux", n_aux, 2 << bit)
            sums = [[(sent, c, 0, small), (got, c, 0, small)] for c in range(chunks)]
        (amp,) = merge([sums], energies=energies, chunks=chunks)
        far_amp, near_amp = swap(amp, "aux", n_aux, far), swap(amp, "aux", n_aux, near)
        both_amp = swap(far_amp, "aux", n_aux, near)
        amps = {
            (0, step, c): (value, (c,))
            for step, value in enumerate([amp, far_amp, near_amp, both_amp])
            for c in range(chunks)
        }
        sources = {(k, part): [streams[2 * part + h][k] for h in range(2)] for k in range(n_occ) for part in range(2)}
        known = {key: value for key, value in amps.items() if key[1] < src_count - 1}
        first = density_first({key: sources[key] for key in early}, known, n_occ, chunks)
        last_sources = [streams[2 * part + h][k] for k, part in late_rows for h in range(2)]
        own = list(amps)
        (packed,) = pack([[amps[key] for key in own]], [first, *spotted(last_sources)[0]])
        arrived = swap(packed, "aux", n_aux, 1)
        for j, (_, step, c) in enumerate(own):
            amps[1, step, c] = (arrived, (j,))
        return density_last(sources, set(early), amps, first, n_occ, chunks)

    in_specs = (P(("aux", "occ"), None, None), P(), P(), P(), P(), P())
    out_specs = P("aux", "occ", None)
    return jax.shard_map(local, mesh=mesh, in_specs=in_specs, out_specs=out_specs, check_vma=False)
```

```python
import functools

import jax
import jax.numpy as jnp
from jax import lax
from jax.experimental import pallas as pl
from jax.experimental.pallas import tpu as pltpu
from jax.sharding import PartitionSpec as P

F32, BF16 = jnp.float32, jnp.bfloat16
MIB = 1 << 20


def swap(value, axis, size, mask):
    return lax.ppermute(value, axis, [(d, d ^ mask) for d in range(size)])


def whole(shape):
    return pl.BlockSpec(shape, lambda *_: (0,) * len(shape))


def chip_mask(src_count):
    chip = lax.axis_index("aux") // 2
    return (chip % 2) * (src_count // 2) + chip // 2 % 2


def prepare_kernel(n_occ, chunks, src_count, src_hbm, x_ref, *refs):
    quarters, src_t, theirs, mine = refs[:4], refs[4], refs[5 : 5 + chunks], refs[5 + chunks : -4]
    arriving, turned, src_ref, arrived = refs[-4:]
    count, step, _, width = arriving.shape
    per_half = src_count // 2
    piece = min(step, quarters[0].shape[0])
    copies = [
        pltpu.make_async_copy(x_ref.at[pl.ds(r * step, step)], arriving.at[r], arrived.at[r]) for r in range(count)
    ]
    src_copy = pltpu.make_async_copy(src_hbm, src_ref, arrived.at[count])
    src_copy.start()
    for copy in copies:
        copy.start()
    src_copy.wait()
    mask = chip_mask(src_count)
    my_occ, core = lax.axis_index("occ"), lax.axis_index("aux") % 2
    for r, copy in enumerate(copies):
        rows = pl.ds(r * step, step)
        copy.wait()
        turned[...] = jnp.swapaxes(arriving[r], 0, 1)
        for s in range(src_count):
            block = turned[src_ref[s ^ mask]]
            for first in range(0, step, piece):
                number, place = divmod(r * step + first, quarters[0].shape[0])
                out, column = quarters[2 * number + s // per_half], s % per_half
                out[pl.ds(place, piece), pl.ds(column * width, width)] = block[first : first + piece]
            src_t[pl.ds(s * width, width), rows] = block.T
        for outs, side in ((theirs, 1 - core), (mine, core)):
            for chunk, out in enumerate(outs):
                for k in range(n_occ):
                    out[k, rows, :] = turned[((k ^ my_occ) * 2 + side) * chunks + chunk]


def prepare(integrals, src, n_occ, chunks):
    rows, occ_count, width = integrals.shape
    src_count = src.shape[0]
    step = min(rows, 128)
    half = src_count * width // 2
    blocks = [(n_occ, rows, width)] * (2 * chunks)
    shapes = [(rows // 2, half)] * 4 + [(src_count * width, rows)] + blocks
    vmem = pl.BlockSpec(memory_space=pltpu.VMEM)
    return pl.pallas_call(
        functools.partial(prepare_kernel, n_occ, chunks, src_count),
        in_specs=[pl.BlockSpec(memory_space=pltpu.HBM)] * 2,
        out_specs=[vmem] * len(shapes),
        out_shape=[jax.ShapeDtypeStruct(s, BF16) for s in shapes],
        scratch_shapes=[
            pltpu.VMEM((rows // step, step, occ_count, width), BF16),
            pltpu.VMEM((occ_count, step, width), BF16),
            pltpu.SMEM((src_count,), jnp.int32),
            pltpu.SemaphoreType.DMA((rows // step + 1,)),
        ],
        cost_estimate=pl.CostEstimate(flops=0, bytes_accessed=0, transcendentals=0),
        compiler_params=pltpu.CompilerParams(vmem_limit_bytes=24 * MIB),
        name="prepare",
    )(*(pltpu.with_memory_space_constraint(v, pltpu.HBM) for v in (src, integrals)))


def pair_both_kernel(pieces, src_own, src_other, ints_own, ints_other, *refs):
    for half, (blocks, out) in enumerate(zip(pieces, refs[-2:], strict=True)):
        tall = out.shape[1]
        rows = pl.ds(half * tall, tall)
        for j, block in enumerate(blocks):
            total = jnp.dot(src_own[rows, :], ints_own[block], preferred_element_type=F32)
            total += jnp.dot(src_other[rows, :], ints_other[block], preferred_element_type=F32)
            out[j] = total.astype(BF16)


def pair_both(src_own, src_other, ints_own, ints_other, pieces, after=()):
    vmem = pl.BlockSpec(memory_space=pltpu.VMEM)
    tall, width = src_own.shape[0] // 2, ints_own.shape[2]
    return pl.pallas_call(
        functools.partial(pair_both_kernel, pieces),
        in_specs=[vmem] * 4 + [pl.BlockSpec(memory_space=pl.ANY)] * len(after),
        out_specs=[vmem] * 2,
        out_shape=[jax.ShapeDtypeStruct((len(blocks), tall, width), BF16) for blocks in pieces],
        compiler_params=pltpu.CompilerParams(vmem_limit_bytes=16 * MIB),
        name="pair_both",
    )(src_own, src_other, ints_own, ints_other, *after)


def pair_kernel(pieces, src_own, src_other, ints_own, ints_other, *refs):
    out = refs[-1]
    tall = out.shape[1]
    for j, (part, block) in enumerate(pieces):
        rows = pl.ds(part * tall, tall)
        total = jnp.dot(src_own[rows, :], ints_own[block], preferred_element_type=F32)
        total += jnp.dot(src_other[rows, :], ints_other[block], preferred_element_type=F32)
        out[j] = total.astype(BF16)


def pair(src_own, src_other, ints_own, ints_other, pieces, parts, after=()):
    vmem = pl.BlockSpec(memory_space=pltpu.VMEM)
    tall, width = src_own.shape[0] // parts, ints_own.shape[2]
    return pl.pallas_call(
        functools.partial(pair_kernel, pieces),
        in_specs=[vmem] * 4 + [pl.BlockSpec(memory_space=pl.ANY)] * len(after),
        out_specs=vmem,
        out_shape=jax.ShapeDtypeStruct((len(pieces), tall, width), BF16),
        compiler_params=pltpu.CompilerParams(vmem_limit_bytes=16 * MIB),
        name="pair",
    )(src_own, src_other, ints_own, ints_other, *after)


def add_terms(refs, terms):
    total = None
    for spot, block, first, count in terms:
        value = refs[spot][block, first : first + count, :].astype(F32)
        total = value if total is None else total + value
    return total


def occupied(chunk, chunks):
    return (lax.axis_index("occ") * 2 + lax.axis_index("aux") % 2) * chunks + chunk


def amplitude(total, place, vir, occ, offset, src):
    first = offset[0]
    row = jnp.broadcast_to(vir[...], total.shape)
    denom = row.T + row - occ[first + place()] - occ[first + src[chip_mask(src.shape[0])]]
    scaled = (total / denom).astype(BF16).astype(F32)
    return 2.0 * scaled - scaled.T


def merge(outputs, energies=None, chunk=0, chunks=1, wide=(), after=(), through=()):
    arrays, places = [], {}

    def spot(array):
        if id(array) not in places:
            places[id(array)] = len(arrays)
            arrays.append(array)
        return places[id(array)]

    plans = [[[(spot(t[0]), *t[1:]) for t in terms] for terms in blocks] for blocks in outputs]
    shapes = [(len(blocks), blocks[0][0][3], blocks[0][0][0].shape[2]) for blocks in outputs]
    extra = [] if energies is None else list(energies)
    n_in = len(arrays) + len(extra)

    def kernel(*refs):
        outs = refs[n_in + len(after) + len(through) :][: len(outputs)]
        for plan, out in zip(plans, outs, strict=True):
            for j, terms in enumerate(plan):
                total = add_terms(refs, terms)
                if energies is not None:
                    total = amplitude(total, functools.partial(occupied, chunk + j, chunks), *refs[len(arrays) : n_in])
                out[j] = total.astype(out.dtype)

    anywhere = pl.BlockSpec(memory_space=pl.ANY)
    vmem, smem = pl.BlockSpec(memory_space=pltpu.VMEM), pl.BlockSpec(memory_space=pltpu.SMEM)
    results = pl.pallas_call(
        kernel,
        in_specs=[vmem] * len(arrays) + [vmem, smem, smem, smem][: len(extra)] + [anywhere] * (len(after) + len(through)),
        out_specs=[vmem] * len(outputs) + [anywhere] * len(through),
        out_shape=[jax.ShapeDtypeStruct(s, F32 if i in wide else BF16) for i, s in enumerate(shapes)]
        + [jax.ShapeDtypeStruct(v.shape, v.dtype) for v in through],
        input_output_aliases={n_in + len(after) + i: len(outputs) + i for i in range(len(through))},
        compiler_params=pltpu.CompilerParams(vmem_limit_bytes=12 * MIB),
        name="merge" if energies is None else "amplitude",
    )(*arrays, *extra, *after, *through)
    return results


def spotted(values):
    arrays, spots = [], []
    for array, index in values:
        same = [array is v for v in arrays]
        if not any(same):
            arrays.append(array)
            same.append(True)
        spots.append((same.index(True), index))
    return arrays, spots


def take(refs, spot):
    number, index = spot
    return refs[number][index] if index else refs[number][...]


def cut(array, index):
    return jax.eval_shape(lambda v: v[index], array).shape


def pack_kernel(spots, sizes, *refs):
    outs = refs[-len(sizes) :]
    for out, size in zip(outs, sizes, strict=True):
        for j in range(size):
            out[j] = take(refs, spots[j])
        spots = spots[size:]


def pack(groups, after=()):
    arrays, spots = spotted([v for group in groups for v in group])
    sizes = [len(group) for group in groups]
    shape = cut(*groups[0][0])
    vmem = pl.BlockSpec(memory_space=pltpu.VMEM)
    return pl.pallas_call(
        functools.partial(pack_kernel, spots, sizes),
        in_specs=[vmem] * len(arrays) + [pl.BlockSpec(memory_space=pl.ANY)] * len(after),
        out_specs=[vmem] * len(groups),
        out_shape=[jax.ShapeDtypeStruct((size, *shape), BF16) for size in sizes],
        compiler_params=pltpu.CompilerParams(vmem_limit_bytes=12 * MIB),
        name="pack",
    )(*arrays, *after)


class Halving:
    def __init__(self, terms, bits, n_occ):
        self.terms, self.bits, self.n_occ = dict(terms), list(bits), n_occ

    def leaving(self):
        return [k for k in sorted(self.terms) if k & self.bits[0]]

    def plan(self):
        return [self.terms[k] for k in self.leaving()]

    def send(self, value):
        leaving, bit = self.leaving(), self.bits.pop(0)
        arrived = swap(value, "occ", self.n_occ, bit)
        for j, k in enumerate(leaving):
            del self.terms[k]
            self.terms[k ^ bit] = self.terms[k ^ bit] + [(arrived, j, 0, value.shape[1])]
        return arrived


def gather_amplitudes(refs, keys, spots, chunks, gathered):
    width = gathered.shape[2]
    for (core, step, chunk), spot in zip(keys, spots, strict=True):
        gathered[core * chunks + chunk, pl.ds(step * width, width), :] = take(refs, spot)


def density_first_kernel(plan, *refs):
    keys, spots, amp_keys = plan
    arrays, (out, gathered) = refs[:-2], refs[-2:]
    chunks, depth, width = gathered.shape
    gather_amplitudes(arrays, amp_keys, spots[2 * len(keys) :], chunks, gathered)
    rows = out.shape[1] // 2
    for place, (k, part) in enumerate(keys):
        halves = [take(arrays, spot) for spot in spots[2 * place : 2 * place + 2]]
        sources = jnp.concatenate(halves, axis=1)[:, :depth]
        for i in range(chunks):
            total = jnp.dot(sources, gathered[i], preferred_element_type=F32)
            out[k, pl.ds(part * rows, rows), pl.ds(i * width, width)] = total


def density_last_kernel(chunks, plan, early, *refs):
    keys, spots, amp_keys = plan
    arrays, first, (out, gathered, turned) = refs[:-4], refs[-4], refs[-3:]
    step = pl.program_id(0)
    depth, width = gathered.shape[1:]
    rows = out.shape[0] // 2
    my_core = lax.axis_index("aux") % 2

    @pl.when(step == 0)
    def _():
        gather_amplitudes(arrays, amp_keys, spots[2 * len(keys) :], chunks, gathered)

    for place, (k, part) in enumerate(keys):

        @pl.when(step == k)
        def _(place=place, k=k, part=part):
            halves = [take(arrays, spot) for spot in spots[2 * place : 2 * place + 2]]
            sources = jnp.concatenate(halves, axis=1)
            mine = slice(part * rows, (part + 1) * rows)
            for core in range(2):
                for chunk in range(chunks):
                    done = depth - width if core == 0 and (k, part) in early else 0
                    amps = gathered[core * chunks + chunk, done:]
                    total = jnp.dot(sources[:, done:], amps, preferred_element_type=F32)
                    if done:
                        total += first[k, mine, chunk * width : (chunk + 1) * width]
                    turned[(my_core if core == 0 else 1 - my_core) * chunks + chunk] = total.astype(BF16)
            out[mine] = jnp.swapaxes(turned[...], 0, 1)


def density_plan(sources, amps):
    values = [v for halves in sources.values() for v in halves]
    arrays, spots = spotted(values + list(amps.values()))
    rows, columns = cut(*values[0])
    return arrays, (list(sources), spots, list(amps)), 2 * rows, 2 * columns


def density_first(sources, amps, n_occ, chunks):
    arrays, plan, rows, columns = density_plan(sources, amps)
    width = cut(*amps[0, 0, 0])[1]
    vmem = pl.BlockSpec(memory_space=pltpu.VMEM)
    return pl.pallas_call(
        functools.partial(density_first_kernel, plan),
        in_specs=[vmem] * len(arrays),
        out_specs=vmem,
        scratch_shapes=[pltpu.VMEM((chunks, columns - width, width), BF16)],
        out_shape=jax.ShapeDtypeStruct((n_occ, rows, chunks * width), F32),
        compiler_params=pltpu.CompilerParams(vmem_limit_bytes=20 * MIB),
        name="density_first",
    )(*arrays)


def density_last(sources, early, amps, first, n_occ, chunks):
    arrays, plan, rows, columns = density_plan(sources, amps)
    width = cut(*amps[0, 0, 0])[1]
    vmem = pl.BlockSpec(memory_space=pltpu.VMEM)
    return pl.pallas_call(
        functools.partial(density_last_kernel, chunks, plan, early),
        grid=(n_occ,),
        in_specs=[vmem] * (len(arrays) + 1),
        out_specs=pl.BlockSpec((rows, 2 * chunks, width), lambda k: (k ^ lax.axis_index("occ"), 0, 0)),
        scratch_shapes=[
            pltpu.VMEM((2 * chunks, columns, width), BF16),
            pltpu.VMEM((2 * chunks, rows // 2, width), BF16),
        ],
        out_shape=jax.ShapeDtypeStruct((n_occ * rows, 2 * chunks, width), BF16),
        compiler_params=pltpu.CompilerParams(vmem_limit_bytes=20 * MIB),
        name="density_last",
    )(*arrays, first)


def solution(mesh):
    n_occ, n_aux = mesh.shape["occ"], mesh.shape["aux"]
    occ_bits = [1 << b for b in range(n_occ.bit_length() - 1)]
    n_chip = n_aux // 2

    def local(integrals, eps_occ, eps_vir, src_occ, occ_offset, vir_offset):
        rows, occ_count, width = integrals.shape
        src_count = src_occ.shape[0]
        owned = occ_count // n_occ
        chunks = owned // 2
        near, far = 2, 4
        low_a, high_a, low_b, high_b, src_t, *ints = prepare(integrals, src_occ, n_occ, chunks)
        theirs, mine = ints[:chunks], ints[chunks:]
        orders = [occ_bits, occ_bits[::-1]] * 2
        streams = [{0: (value, ())} for value in (low_a, high_a, low_b, high_b)]
        for order, have in zip(orders[:2], streams[:2], strict=True):
            have[order[0]] = (swap(have[0][0], "occ", n_occ, order[0]), ())
        ahead = [have[order[0]][0] for order, have in zip(orders[:2], streams[:2], strict=True)]

        def leaving_sources():
            groups = {}
            for number, (order, have) in enumerate(zip(orders, streams, strict=True)):
                blocks = [0]
                for bit in order:
                    wanted = [(number, k) for k in blocks if k in have and k | bit not in have]
                    if wanted:
                        groups.setdefault(bit, []).extend(wanted)
                    blocks = blocks + [k | bit for k in blocks]
            return groups

        def pack_sources(groups, after=()):
            return pack([[streams[number][k] for number, k in group] for group in groups.values()], after)

        def send_sources(groups, packs):
            arrived = [swap(packed, "occ", n_occ, bit) for bit, packed in zip(groups, packs, strict=True)]
            for (bit, group), array in zip(groups.items(), arrived, strict=True):
                for j, (number, k) in enumerate(group):
                    streams[number][k | bit] = (array, (j,))

        src_other = swap(src_t, "aux", n_aux, 1)
        other = [None] * chunks
        for c in reversed(range(chunks)):
            other[c] = swap(theirs[c], "aux", n_aux, 1)

        vir_energy = lax.dynamic_slice_in_dim(eps_vir, vir_offset[0], width).reshape(1, width)

        def product(c, parts, pieces, after=()):
            return pair(src_t, src_other, mine[c], other[c], pieces, parts, after)

        tall = src_count // 2 * width
        small = tall // 2
        half_n = n_occ // 2
        even, odd = list(range(0, n_occ, 2)), list(range(1, n_occ, 2))
        front, back = list(range(half_n)), list(range(half_n, n_occ))
        near_pieces = [
            [(2, k) for k in odd] + [(3, k) for k in back],
            [(2, k) for k in even] + [(3, k) for k in front],
        ]
        near_sent = product(1, 4, near_pieces[0])
        near_got = [swap(near_sent, "aux", n_aux, near)]
        sent_x = product(0, 2, [(0, k) for k in odd], [near_sent])
        sent_y = product(0, 2, [(1, k) for k in back], [near_sent, *ahead])
        near_got.append(swap(product(1, 4, near_pieces[1], [sent_x, sent_y]), "aux", n_aux, near))
        groups = leaving_sources()
        packs = pack_sources(groups)
        held = [near_got[0]]
        kept_x, kept_y = pair_both(src_t, src_other, mine[0], other[0], (even, front), held)
        first_x = {2 * i: [(kept_x, i, 0, tall)] for i in range(half_n)}
        first_x |= {2 * i + 1: [(sent_x, i, 0, tall)] for i in range(half_n)}
        first_y = {i: [(kept_y, i, 0, tall)] for i in range(half_n)}
        first_y |= {half_n + i: [(sent_y, i, 0, tall)] for i in range(half_n)}
        unit_x, unit_y = Halving(first_x, occ_bits, n_occ), Halving(first_y, occ_bits[::-1], n_occ)
        got_x, got_y = unit_x.send(sent_x), unit_y.send(sent_y)
        while unit_x.bits:
            sent_x, sent_y = merge([unit_x.plan(), unit_y.plan()])
            got_x, got_y = unit_x.send(sent_x), unit_y.send(sent_y)
        near_kept = product(1, 2, [(0, k) for k in range(n_occ)], [kept_x, kept_y])
        (sent,) = merge([[unit_y.terms[0]]], after=[got_x])
        got = swap(sent, "aux", n_aux, near)
        terms_0 = unit_x.terms[0] + [(got, 0, 0, tall)]

        def rows_of(terms, first, count):
            return [(array, block, start + first, count) for array, block, start, _ in terms]

        both = [{k: [(near_kept, k, small * part, small)] for k in range(n_occ)} for part in range(2)]
        for got, pieces in zip(near_got, near_pieces, strict=True):
            for j, (part, k) in enumerate(pieces):
                both[part - 2][k].append((got, j, 0, small))
        unit_x, unit_y = Halving(both[0], occ_bits, n_occ), Halving(both[1], occ_bits[::-1], n_occ)
        sent_x, sent_y = merge([unit_x.plan(), unit_y.plan()], after=[])
        got_x, got_y = unit_x.send(sent_x), unit_y.send(sent_y)

        sent_0, kept_0 = merge([[rows_of(terms_0, small, small)], [rows_of(terms_0, 0, small)]], wide=[1])
        got_0 = swap(sent_0, "aux", n_aux, far)
        terms_0 = [(kept_0, 0, 0, small), (got_0, 0, 0, small)]

        while unit_x.bits:
            sent_x, sent_y = merge([unit_x.plan(), unit_y.plan()])
            got_x, got_y = unit_x.send(sent_x), unit_y.send(sent_y)
        sent_1, kept_1, *packs = merge(
            [[unit_y.terms[0]], [unit_x.terms[0]]], wide=[1], after=[sent_0], through=packs
        )
        got_1 = swap(sent_1, "aux", n_aux, far)
        terms_1 = [(kept_1, 0, 0, small), (got_1, 0, 0, small)]

        send_sources(groups, packs)
        while groups := leaving_sources():
            soon = [dict(have) for have in streams]
            send_sources(groups, pack_sources(groups))
        early = [(k, part) for k in range(n_occ) for part in range(2)]
        late_rows = []

        energies = [vir_energy, eps_occ, occ_offset, src_occ]
        sums = [terms_0, terms_1]
        for bit in range(2, n_chip.bit_length() - 1):
            (sent,) = merge([sums])
            got = swap(sent, "aux", n_aux, 2 << bit)
            sums = [[(sent, c, 0, small), (got, c, 0, small)] for c in range(chunks)]
        (amp,) = merge([sums], energies=energies, chunks=chunks)
        far_amp, near_amp = swap(amp, "aux", n_aux, far), swap(amp, "aux", n_aux, near)
        both_amp = swap(far_amp, "aux", n_aux, near)
        amps = {
            (0, step, c): (value, (c,))
            for step, value in enumerate([amp, far_amp, near_amp, both_amp])
            for c in range(chunks)
        }
        sources = {(k, part): [streams[2 * part + h][k] for h in range(2)] for k in range(n_occ) for part in range(2)}
        known = {key: value for key, value in amps.items() if key[1] < src_count - 1}
        first = density_first({key: sources[key] for key in early}, known, n_occ, chunks)
        last_sources = [streams[2 * part + h][k] for k, part in late_rows for h in range(2)]
        own = list(amps)
        (packed,) = pack([[amps[key] for key in own]], [first, *spotted(last_sources)[0]])
        arrived = swap(packed, "aux", n_aux, 1)
        for j, (_, step, c) in enumerate(own):
            amps[1, step, c] = (arrived, (j,))
        return density_last(sources, set(early), amps, first, n_occ, chunks)

    in_specs = (P(("aux", "occ"), None, None), P(), P(), P(), P(), P())
    out_specs = P("aux", "occ", None)
    return jax.shard_map(local, mesh=mesh, in_specs=in_specs, out_specs=out_specs, check_vma=False)
```

```python
import functools

import jax
import jax.numpy as jnp
from jax import lax
from jax.experimental import pallas as pl
from jax.experimental.pallas import tpu as pltpu
from jax.sharding import PartitionSpec as P

F32, BF16 = jnp.float32, jnp.bfloat16
MIB = 1 << 20


def swap(value, axis, size, mask):
    return lax.ppermute(value, axis, [(d, d ^ mask) for d in range(size)])


def whole(shape):
    return pl.BlockSpec(shape, lambda *_: (0,) * len(shape))


def chip_mask(src_count):
    chip = lax.axis_index("aux") // 2
    return (chip % 2) * (src_count // 2) + chip // 2 % 2


def prepare_kernel(n_occ, chunks, src_count, src_hbm, x_ref, *refs):
    quarters, src_t, theirs, mine = refs[:4], refs[4], refs[5 : 5 + chunks], refs[5 + chunks : -4]
    arriving, turned, src_ref, arrived = refs[-4:]
    count, step, _, width = arriving.shape
    per_half = src_count // 2
    piece = min(step, quarters[0].shape[0])
    copies = [
        pltpu.make_async_copy(x_ref.at[pl.ds(r * step, step)], arriving.at[r], arrived.at[r]) for r in range(count)
    ]
    src_copy = pltpu.make_async_copy(src_hbm, src_ref, arrived.at[count])
    src_copy.start()
    for copy in copies:
        copy.start()
    src_copy.wait()
    mask = chip_mask(src_count)
    my_occ, core = lax.axis_index("occ"), lax.axis_index("aux") % 2
    for r, copy in enumerate(copies):
        rows = pl.ds(r * step, step)
        copy.wait()
        turned[...] = jnp.swapaxes(arriving[r], 0, 1)
        for s in range(src_count):
            block = turned[src_ref[s ^ mask]]
            for first in range(0, step, piece):
                number, place = divmod(r * step + first, quarters[0].shape[0])
                out, column = quarters[2 * number + s // per_half], s % per_half
                out[pl.ds(place, piece), pl.ds(column * width, width)] = block[first : first + piece]
            src_t[pl.ds(s * width, width), rows] = block.T
        for outs, side in ((theirs, 1 - core), (mine, core)):
            for chunk, out in enumerate(outs):
                for k in range(n_occ):
                    out[k, rows, :] = turned[((k ^ my_occ) * 2 + side) * chunks + chunk]


def prepare(integrals, src, n_occ, chunks):
    rows, occ_count, width = integrals.shape
    src_count = src.shape[0]
    step = min(rows, 128)
    half = src_count * width // 2
    blocks = [(n_occ, rows, width)] * (2 * chunks)
    shapes = [(rows // 2, half)] * 4 + [(src_count * width, rows)] + blocks
    vmem = pl.BlockSpec(memory_space=pltpu.VMEM)
    return pl.pallas_call(
        functools.partial(prepare_kernel, n_occ, chunks, src_count),
        in_specs=[pl.BlockSpec(memory_space=pltpu.HBM)] * 2,
        out_specs=[vmem] * len(shapes),
        out_shape=[jax.ShapeDtypeStruct(s, BF16) for s in shapes],
        scratch_shapes=[
            pltpu.VMEM((rows // step, step, occ_count, width), BF16),
            pltpu.VMEM((occ_count, step, width), BF16),
            pltpu.SMEM((src_count,), jnp.int32),
            pltpu.SemaphoreType.DMA((rows // step + 1,)),
        ],
        cost_estimate=pl.CostEstimate(flops=0, bytes_accessed=0, transcendentals=0),
        compiler_params=pltpu.CompilerParams(vmem_limit_bytes=24 * MIB),
        name="prepare",
    )(*(pltpu.with_memory_space_constraint(v, pltpu.HBM) for v in (src, integrals)))


def pair_both_kernel(pieces, src_own, src_other, ints_own, ints_other, *refs):
    for half, (blocks, out) in enumerate(zip(pieces, refs[-2:], strict=True)):
        tall = out.shape[1]
        rows = pl.ds(half * tall, tall)
        for j, block in enumerate(blocks):
            total = jnp.dot(src_own[rows, :], ints_own[block], preferred_element_type=F32)
            total += jnp.dot(src_other[rows, :], ints_other[block], preferred_element_type=F32)
            out[j] = total.astype(BF16)


def pair_both(src_own, src_other, ints_own, ints_other, pieces, after=()):
    vmem = pl.BlockSpec(memory_space=pltpu.VMEM)
    tall, width = src_own.shape[0] // 2, ints_own.shape[2]
    return pl.pallas_call(
        functools.partial(pair_both_kernel, pieces),
        in_specs=[vmem] * 4 + [pl.BlockSpec(memory_space=pl.ANY)] * len(after),
        out_specs=[vmem] * 2,
        out_shape=[jax.ShapeDtypeStruct((len(blocks), tall, width), BF16) for blocks in pieces],
        compiler_params=pltpu.CompilerParams(vmem_limit_bytes=16 * MIB),
        name="pair_both",
    )(src_own, src_other, ints_own, ints_other, *after)


def pair_kernel(pieces, src_own, src_other, ints_own, ints_other, *refs):
    out = refs[-1]
    tall = out.shape[1]
    for j, (part, block) in enumerate(pieces):
        rows = pl.ds(part * tall, tall)
        total = jnp.dot(src_own[rows, :], ints_own[block], preferred_element_type=F32)
        total += jnp.dot(src_other[rows, :], ints_other[block], preferred_element_type=F32)
        out[j] = total.astype(BF16)


def pair(src_own, src_other, ints_own, ints_other, pieces, parts, after=()):
    vmem = pl.BlockSpec(memory_space=pltpu.VMEM)
    tall, width = src_own.shape[0] // parts, ints_own.shape[2]
    return pl.pallas_call(
        functools.partial(pair_kernel, pieces),
        in_specs=[vmem] * 4 + [pl.BlockSpec(memory_space=pl.ANY)] * len(after),
        out_specs=vmem,
        out_shape=jax.ShapeDtypeStruct((len(pieces), tall, width), BF16),
        compiler_params=pltpu.CompilerParams(vmem_limit_bytes=16 * MIB),
        name="pair",
    )(src_own, src_other, ints_own, ints_other, *after)


def add_terms(refs, terms):
    total = None
    for spot, block, first, count in terms:
        value = refs[spot][block, first : first + count, :].astype(F32)
        total = value if total is None else total + value
    return total


def occupied(chunk, chunks):
    return (lax.axis_index("occ") * 2 + lax.axis_index("aux") % 2) * chunks + chunk


def amplitude(total, place, vir, occ, offset, src):
    first = offset[0]
    row = jnp.broadcast_to(vir[...], total.shape)
    denom = row.T + row - occ[first + place()] - occ[first + src[chip_mask(src.shape[0])]]
    scaled = (total / denom).astype(BF16).astype(F32)
    return 2.0 * scaled - scaled.T


def merge(outputs, energies=None, chunk=0, chunks=1, wide=(), after=(), through=()):
    arrays, places = [], {}

    def spot(array):
        if id(array) not in places:
            places[id(array)] = len(arrays)
            arrays.append(array)
        return places[id(array)]

    plans = [[[(spot(t[0]), *t[1:]) for t in terms] for terms in blocks] for blocks in outputs]
    shapes = [(len(blocks), blocks[0][0][3], blocks[0][0][0].shape[2]) for blocks in outputs]
    extra = [] if energies is None else list(energies)
    n_in = len(arrays) + len(extra)

    def kernel(*refs):
        outs = refs[n_in + len(after) + len(through) :][: len(outputs)]
        for plan, out in zip(plans, outs, strict=True):
            for j, terms in enumerate(plan):
                total = add_terms(refs, terms)
                if energies is not None:
                    total = amplitude(total, functools.partial(occupied, chunk + j, chunks), *refs[len(arrays) : n_in])
                out[j] = total.astype(out.dtype)

    anywhere = pl.BlockSpec(memory_space=pl.ANY)
    vmem, smem = pl.BlockSpec(memory_space=pltpu.VMEM), pl.BlockSpec(memory_space=pltpu.SMEM)
    results = pl.pallas_call(
        kernel,
        in_specs=[vmem] * len(arrays) + [vmem, smem, smem, smem][: len(extra)] + [anywhere] * (len(after) + len(through)),
        out_specs=[vmem] * len(outputs) + [anywhere] * len(through),
        out_shape=[jax.ShapeDtypeStruct(s, F32 if i in wide else BF16) for i, s in enumerate(shapes)]
        + [jax.ShapeDtypeStruct(v.shape, v.dtype) for v in through],
        input_output_aliases={n_in + len(after) + i: len(outputs) + i for i in range(len(through))},
        compiler_params=pltpu.CompilerParams(vmem_limit_bytes=12 * MIB),
        name="merge" if energies is None else "amplitude",
    )(*arrays, *extra, *after, *through)
    return results


def spotted(values):
    arrays, spots = [], []
    for array, index in values:
        same = [array is v for v in arrays]
        if not any(same):
            arrays.append(array)
            same.append(True)
        spots.append((same.index(True), index))
    return arrays, spots


def take(refs, spot):
    number, index = spot
    return refs[number][index] if index else refs[number][...]


def cut(array, index):
    return jax.eval_shape(lambda v: v[index], array).shape


def pack_kernel(spots, sizes, *refs):
    outs = refs[-len(sizes) :]
    for out, size in zip(outs, sizes, strict=True):
        for j in range(size):
            out[j] = take(refs, spots[j])
        spots = spots[size:]


def pack(groups, after=()):
    arrays, spots = spotted([v for group in groups for v in group])
    sizes = [len(group) for group in groups]
    shape = cut(*groups[0][0])
    vmem = pl.BlockSpec(memory_space=pltpu.VMEM)
    return pl.pallas_call(
        functools.partial(pack_kernel, spots, sizes),
        in_specs=[vmem] * len(arrays) + [pl.BlockSpec(memory_space=pl.ANY)] * len(after),
        out_specs=[vmem] * len(groups),
        out_shape=[jax.ShapeDtypeStruct((size, *shape), BF16) for size in sizes],
        compiler_params=pltpu.CompilerParams(vmem_limit_bytes=12 * MIB),
        name="pack",
    )(*arrays, *after)


class Halving:
    def __init__(self, terms, bits, n_occ):
        self.terms, self.bits, self.n_occ = dict(terms), list(bits), n_occ

    def leaving(self):
        return [k for k in sorted(self.terms) if k & self.bits[0]]

    def plan(self):
        return [self.terms[k] for k in self.leaving()]

    def send(self, value):
        leaving, bit = self.leaving(), self.bits.pop(0)
        arrived = swap(value, "occ", self.n_occ, bit)
        for j, k in enumerate(leaving):
            del self.terms[k]
            self.terms[k ^ bit] = self.terms[k ^ bit] + [(arrived, j, 0, value.shape[1])]
        return arrived


def gather_amplitudes(refs, keys, spots, chunks, gathered):
    width = gathered.shape[2]
    for (core, step, chunk), spot in zip(keys, spots, strict=True):
        gathered[core * chunks + chunk, pl.ds(step * width, width), :] = take(refs, spot)


def density_first_kernel(plan, *refs):
    keys, spots, amp_keys = plan
    arrays, (out, gathered) = refs[:-2], refs[-2:]
    chunks, depth, width = gathered.shape
    gather_amplitudes(arrays, amp_keys, spots[2 * len(keys) :], chunks, gathered)
    rows = out.shape[1] // 2
    for place, (k, part) in enumerate(keys):
        halves = [take(arrays, spot) for spot in spots[2 * place : 2 * place + 2]]
        sources = jnp.concatenate(halves, axis=1)[:, :depth]
        for i in range(chunks):
            total = jnp.dot(sources, gathered[i], preferred_element_type=F32)
            out[k, pl.ds(part * rows, rows), pl.ds(i * width, width)] = total


def density_last_kernel(chunks, plan, *refs):
    keys, spots, amp_keys = plan
    arrays, first, (out, gathered, turned) = refs[:-4], refs[-4], refs[-3:]
    step = pl.program_id(0)
    depth, width = gathered.shape[1:]
    my_core = lax.axis_index("aux") % 2

    @pl.when(step == 0)
    def _():
        gather_amplitudes(arrays, amp_keys, spots[2 * len(keys) :], chunks, gathered)

    for k in range(len(keys) // 2):

        @pl.when(step == k)
        def _(k=k):
            quarters = [take(arrays, spot) for spot in spots[4 * k : 4 * k + 4]]
            halves = [jnp.concatenate(quarters[2 * part : 2 * part + 2], axis=1) for part in range(2)]
            sources = jnp.concatenate(halves, axis=0)
            for core in range(2):
                for chunk in range(chunks):
                    done = depth - width if core == 0 else 0
                    amps = gathered[core * chunks + chunk, done:]
                    total = jnp.dot(sources[:, done:], amps, preferred_element_type=F32)
                    if done:
                        total += first[k, :, chunk * width : (chunk + 1) * width]
                    turned[(my_core if core == 0 else 1 - my_core) * chunks + chunk] = total.astype(BF16)
            out[...] = jnp.swapaxes(turned[...], 0, 1)


def density_plan(sources, amps):
    values = [v for halves in sources.values() for v in halves]
    arrays, spots = spotted(values + list(amps.values()))
    rows, columns = cut(*values[0])
    return arrays, (list(sources), spots, list(amps)), 2 * rows, 2 * columns


def density_first(sources, amps, n_occ, chunks):
    arrays, plan, rows, columns = density_plan(sources, amps)
    width = cut(*amps[0, 0, 0])[1]
    vmem = pl.BlockSpec(memory_space=pltpu.VMEM)
    return pl.pallas_call(
        functools.partial(density_first_kernel, plan),
        in_specs=[vmem] * len(arrays),
        out_specs=vmem,
        scratch_shapes=[pltpu.VMEM((chunks, columns - width, width), BF16)],
        out_shape=jax.ShapeDtypeStruct((n_occ, rows, chunks * width), F32),
        compiler_params=pltpu.CompilerParams(vmem_limit_bytes=20 * MIB),
        name="density_first",
    )(*arrays)


def density_last(sources, amps, first, n_occ, chunks):
    arrays, plan, rows, columns = density_plan(sources, amps)
    width = cut(*amps[0, 0, 0])[1]
    vmem = pl.BlockSpec(memory_space=pltpu.VMEM)
    return pl.pallas_call(
        functools.partial(density_last_kernel, chunks, plan),
        grid=(n_occ,),
        in_specs=[vmem] * (len(arrays) + 1),
        out_specs=pl.BlockSpec((rows, 2 * chunks, width), lambda k: (k ^ lax.axis_index("occ"), 0, 0)),
        scratch_shapes=[
            pltpu.VMEM((2 * chunks, columns, width), BF16),
            pltpu.VMEM((2 * chunks, rows, width), BF16),
        ],
        out_shape=jax.ShapeDtypeStruct((n_occ * rows, 2 * chunks, width), BF16),
        compiler_params=pltpu.CompilerParams(vmem_limit_bytes=20 * MIB),
        name="density_last",
    )(*arrays, first)


def solution(mesh):
    n_occ, n_aux = mesh.shape["occ"], mesh.shape["aux"]
    occ_bits = [1 << b for b in range(n_occ.bit_length() - 1)]
    n_chip = n_aux // 2

    def local(integrals, eps_occ, eps_vir, src_occ, occ_offset, vir_offset):
        rows, occ_count, width = integrals.shape
        src_count = src_occ.shape[0]
        owned = occ_count // n_occ
        chunks = owned // 2
        near, far = 2, 4
        low_a, high_a, low_b, high_b, src_t, *ints = prepare(integrals, src_occ, n_occ, chunks)
        theirs, mine = ints[:chunks], ints[chunks:]
        orders = [occ_bits, occ_bits[::-1]] * 2
        streams = [{0: (value, ())} for value in (low_a, high_a, low_b, high_b)]
        for order, have in zip(orders[:2], streams[:2], strict=True):
            have[order[0]] = (swap(have[0][0], "occ", n_occ, order[0]), ())
        ahead = [have[order[0]][0] for order, have in zip(orders[:2], streams[:2], strict=True)]

        def leaving_sources():
            groups = {}
            for number, (order, have) in enumerate(zip(orders, streams, strict=True)):
                blocks = [0]
                for bit in order:
                    wanted = [(number, k) for k in blocks if k in have and k | bit not in have]
                    if wanted:
                        groups.setdefault(bit, []).extend(wanted)
                    blocks = blocks + [k | bit for k in blocks]
            return groups

        def pack_sources(groups, after=()):
            return pack([[streams[number][k] for number, k in group] for group in groups.values()], after)

        def send_sources(groups, packs):
            arrived = [swap(packed, "occ", n_occ, bit) for bit, packed in zip(groups, packs, strict=True)]
            for (bit, group), array in zip(groups.items(), arrived, strict=True):
                for j, (number, k) in enumerate(group):
                    streams[number][k | bit] = (array, (j,))

        src_other = swap(src_t, "aux", n_aux, 1)
        other = [None] * chunks
        for c in reversed(range(chunks)):
            other[c] = swap(theirs[c], "aux", n_aux, 1)

        vir_energy = lax.dynamic_slice_in_dim(eps_vir, vir_offset[0], width).reshape(1, width)

        def product(c, parts, pieces, after=()):
            return pair(src_t, src_other, mine[c], other[c], pieces, parts, after)

        tall = src_count // 2 * width
        small = tall // 2
        half_n = n_occ // 2
        even, odd = list(range(0, n_occ, 2)), list(range(1, n_occ, 2))
        front, back = list(range(half_n)), list(range(half_n, n_occ))
        near_pieces = [
            [(2, k) for k in odd] + [(3, k) for k in back],
            [(2, k) for k in even] + [(3, k) for k in front],
        ]
        near_sent = product(1, 4, near_pieces[0])
        near_got = [swap(near_sent, "aux", n_aux, near)]
        sent_x = product(0, 2, [(0, k) for k in odd], [near_sent])
        sent_y = product(0, 2, [(1, k) for k in back], [near_sent, *ahead])
        near_got.append(swap(product(1, 4, near_pieces[1], [sent_x, sent_y]), "aux", n_aux, near))
        groups = leaving_sources()
        packs = pack_sources(groups)
        held = [near_got[0]]
        kept_x, kept_y = pair_both(src_t, src_other, mine[0], other[0], (even, front), held)
        first_x = {2 * i: [(kept_x, i, 0, tall)] for i in range(half_n)}
        first_x |= {2 * i + 1: [(sent_x, i, 0, tall)] for i in range(half_n)}
        first_y = {i: [(kept_y, i, 0, tall)] for i in range(half_n)}
        first_y |= {half_n + i: [(sent_y, i, 0, tall)] for i in range(half_n)}
        unit_x, unit_y = Halving(first_x, occ_bits, n_occ), Halving(first_y, occ_bits[::-1], n_occ)
        got_x, got_y = unit_x.send(sent_x), unit_y.send(sent_y)
        while unit_x.bits:
            sent_x, sent_y = merge([unit_x.plan(), unit_y.plan()])
            got_x, got_y = unit_x.send(sent_x), unit_y.send(sent_y)
        near_kept = product(1, 2, [(0, k) for k in range(n_occ)], [kept_x, kept_y])
        (sent,) = merge([[unit_y.terms[0]]], after=[got_x])
        got = swap(sent, "aux", n_aux, near)
        terms_0 = unit_x.terms[0] + [(got, 0, 0, tall)]

        def rows_of(terms, first, count):
            return [(array, block, start + first, count) for array, block, start, _ in terms]

        both = [{k: [(near_kept, k, small * part, small)] for k in range(n_occ)} for part in range(2)]
        for got, pieces in zip(near_got, near_pieces, strict=True):
            for j, (part, k) in enumerate(pieces):
                both[part - 2][k].append((got, j, 0, small))
        unit_x, unit_y = Halving(both[0], occ_bits, n_occ), Halving(both[1], occ_bits[::-1], n_occ)
        sent_x, sent_y = merge([unit_x.plan(), unit_y.plan()], after=[])
        got_x, got_y = unit_x.send(sent_x), unit_y.send(sent_y)

        sent_0, kept_0 = merge([[rows_of(terms_0, small, small)], [rows_of(terms_0, 0, small)]], wide=[1])
        got_0 = swap(sent_0, "aux", n_aux, far)
        terms_0 = [(kept_0, 0, 0, small), (got_0, 0, 0, small)]

        while unit_x.bits:
            sent_x, sent_y = merge([unit_x.plan(), unit_y.plan()])
            got_x, got_y = unit_x.send(sent_x), unit_y.send(sent_y)
        sent_1, kept_1, *packs = merge(
            [[unit_y.terms[0]], [unit_x.terms[0]]], wide=[1], after=[sent_0], through=packs
        )
        got_1 = swap(sent_1, "aux", n_aux, far)
        terms_1 = [(kept_1, 0, 0, small), (got_1, 0, 0, small)]

        send_sources(groups, packs)
        while groups := leaving_sources():
            soon = [dict(have) for have in streams]
            send_sources(groups, pack_sources(groups))
        early = [(k, part) for k in range(n_occ) for part in range(2)]
        late_rows = []

        energies = [vir_energy, eps_occ, occ_offset, src_occ]
        sums = [terms_0, terms_1]
        for bit in range(2, n_chip.bit_length() - 1):
            (sent,) = merge([sums])
            got = swap(sent, "aux", n_aux, 2 << bit)
            sums = [[(sent, c, 0, small), (got, c, 0, small)] for c in range(chunks)]
        (amp,) = merge([sums], energies=energies, chunks=chunks)
        far_amp, near_amp = swap(amp, "aux", n_aux, far), swap(amp, "aux", n_aux, near)
        both_amp = swap(far_amp, "aux", n_aux, near)
        amps = {
            (0, step, c): (value, (c,))
            for step, value in enumerate([amp, far_amp, near_amp, both_amp])
            for c in range(chunks)
        }
        sources = {(k, part): [streams[2 * part + h][k] for h in range(2)] for k in range(n_occ) for part in range(2)}
        known = {key: value for key, value in amps.items() if key[1] < src_count - 1}
        first = density_first({key: sources[key] for key in early}, known, n_occ, chunks)
        last_sources = [streams[2 * part + h][k] for k, part in late_rows for h in range(2)]
        own = list(amps)
        (packed,) = pack([[amps[key] for key in own]], [first, *spotted(last_sources)[0]])
        arrived = swap(packed, "aux", n_aux, 1)
        for j, (_, step, c) in enumerate(own):
            amps[1, step, c] = (arrived, (j,))
        return density_last(sources, amps, first, n_occ, chunks)

    in_specs = (P(("aux", "occ"), None, None), P(), P(), P(), P(), P())
    out_specs = P("aux", "occ", None)
    return jax.shard_map(local, mesh=mesh, in_specs=in_specs, out_specs=out_specs, check_vma=False)
```
